256 devices in a mesh: dp: 2 (over core), seq: 16 (over z_lo, x), chan: 8 (over y, z_hi).
Axes of the slice: x: 4, y: 4, z: 8 (z_hi: 2, z_lo: 4; z = z_hi * 4 + z_lo), core: 2. Of those that a mesh axis runs over, the one named last changes fastest.
Arguments:
- tokens: bfloat16 [1, 8192, 4096], P(None, ('dp', 'seq'), 'chan'), may hold values from -6 to 6
- w_value: bfloat16 [4096, 4096], P(None, 'chan'), may hold values from -0.09375 to 0.09375
- gate_k: bfloat16 [1, 8192, 4096], P(None, ('dp', 'seq'), 'chan'), may hold values from -5 to 5
- gate_q: bfloat16 [1, 8192, 4096], P(None, ('dp', 'seq'), 'chan'), may hold values from -5 to 5
- filter_weight: float32 [64, 4096], P(None, 'chan'), may hold values from -6 to 6
- decay: float32 [4096], P('chan'), may hold values from 0.5 to 8
- skip_bias: float32 [4096], P('chan'), may hold values from 0.5 to 1.5
- cotangent: bfloat16 [1, 8192, 4096], P(None, ('dp', 'seq'), 'chan'), may hold values from -16 to 16
Outputs:
- mixed: bfloat16 [1, 8192, 4096], P(None, ('dp', 'seq'), 'chan')
- grad_tokens: bfloat16 [1, 8192, 4096], P(None, ('dp', 'seq'), 'chan')
- grad_gate_k: bfloat16 [1, 8192, 4096], P(None, ('dp', 'seq'), 'chan')
- grad_gate_q: bfloat16 [1, 8192, 4096], P(None, ('dp', 'seq'), 'chan')
- grad_filter: float32 [64, 4096], P(None, 'chan')
- grad_bias: float32 [4096], P('chan')
The draws below stay inside these ranges and needn't reach their ends.
All inputs are finite; a program needn't handle non-finite values.
Results may differ from the reference program's by a relative error of at most 0.012.
Values may be sent and summed in bfloat16 or wider, within the bound.
A program may use at most 128 MiB of HBM per device.

```python
import math
import jax
import jax.numpy as jnp
from jax import lax

D = 4096
ORDER = 64
L = 8192
STREAMS = 1


def draw_cotangent(key, part):
    key = jax.random.fold_in(key, 11)
    position = jnp.arange(L, dtype=jnp.float32) / max(L - 1, 1)
    base = jax.random.truncated_normal(key, -4.0, 4.0, (STREAMS, L, D), jnp.float32)
    growth = 1.0 + 2.0 * position
    return (base * growth[None, :, None]).astype(jnp.bfloat16)


def level_of(stream_key, extent, split, low, high):
    gain = 1.0
    for dim, parts in split:
        draws = jax.random.uniform(jax.random.fold_in(jax.random.fold_in(stream_key, 6), dim), (parts,), jnp.float32, low / len(split), high / len(split))
        gain = gain * jnp.repeat(jnp.exp(draws), extent[dim] // parts).reshape((-1,) + (1,) * (len(extent) - 1 - dim))
    return gain


def centred(own_key, shape, deviation, most, split=(), held_as=jnp.bfloat16):
    factor_of = level_of(own_key, shape, split, -0.22, 0.18) if split else 1.0
    array = jax.random.normal(own_key, shape, jnp.float32) * deviation * factor_of
    return jnp.minimum(jnp.maximum(array, -most), most).astype(held_as)


def setup_inputs(seed: int = 0) -> dict:
    keys = jax.random.split(jax.random.key(seed), 9)
    return {
        "tokens": centred(keys[0], (STREAMS, L, D), 1.0, 6.0, ((1, 32), (2, 8))),
        "w_value": centred(keys[1], (D, D), D ** -0.5, 0.09375, ((1, 8),)),
        "gate_k": centred(keys[2], (STREAMS, L, D), 1.0, 5.0, ((1, 32), (2, 8))),
        "gate_q": centred(keys[3], (STREAMS, L, D), 1.0, 5.0, ((1, 32), (2, 8))),
        "filter_weight": centred(keys[4], (ORDER, D), 1.0, 6.0, ((1, 8),), jnp.float32),
        "decay": jnp.clip(jnp.exp(math.log(8.0) - 2.7725887 * jax.random.uniform(keys[5], (D,), jnp.float32) ** level_of(keys[5], (D,), ((0, 8),), -0.2, 0.2)), 0.5, 8.0),
        "skip_bias": jnp.clip(0.5 + 1.0 * jax.random.uniform(keys[6], (D,), jnp.float32) ** level_of(keys[6], (D,), ((0, 8),), -0.2, 0.2), 0.5, 1.5),
        "cotangent": draw_cotangent(jax.random.fold_in(keys[8], 71), 0),
    }


def filter_basis(length, filter_order):
    positions = jnp.arange(length, dtype=jnp.int32)
    harmonics = jnp.arange(1, filter_order + 1, dtype=jnp.int32)
    period = 4 * filter_order
    phases = positions[:, None] * harmonics[None, :] % period
    return jnp.cos(2.0 * math.pi / period * phases.astype(jnp.float32))

def reference(tokens, w_value, gate_k, gate_q, filter_weight, decay, skip_bias, cotangent):
    exact_mode = lax.Precision.HIGHEST
    length = L
    padded = 2 * length
    cosines = filter_basis(length, ORDER)
    steps_frac = jnp.arange(length, dtype=jnp.float32) / length
    fading = jnp.exp(-steps_frac[:, None] * decay[None, :])
    kernel_scale = 1.0 / math.sqrt(ORDER * length)
    kernel = fading * jnp.dot(cosines, filter_weight, precision=exact_mode) * kernel_scale
    kernel_spec = jnp.fft.rfft(kernel, n=padded, axis=0)

    def per_stream(operands):
        tok_rows, key_rows, query_rows, incoming_bf = operands
        values_bf = jnp.dot(tok_rows, w_value, preferred_element_type=jnp.float32).astype(jnp.bfloat16)
        key_gate = key_rows.astype(jnp.float32)
        query_gate = query_rows.astype(jnp.float32)
        mixed_in = key_gate * values_bf.astype(jnp.float32)
        input_spec = jnp.fft.rfft(mixed_in, n=padded, axis=0)
        convolved = jnp.fft.irfft(input_spec * kernel_spec, n=padded, axis=0)[:length]
        gated_state = convolved + skip_bias[None, :] * mixed_in
        mixed_out = (query_gate * gated_state).astype(jnp.bfloat16)
        incoming = incoming_bf.astype(jnp.float32)
        grad_state = query_gate * incoming
        grad_spec = jnp.fft.rfft(grad_state, n=padded, axis=0)
        grad_in = jnp.fft.irfft(jnp.conj(kernel_spec) * grad_spec, n=padded, axis=0)[:length]
        grad_in = grad_in + skip_bias[None, :] * grad_state
        grad_kernel = jnp.fft.irfft(jnp.conj(input_spec) * grad_spec, n=padded, axis=0)[:length]
        grad_values = (key_gate * grad_in).astype(jnp.bfloat16)
        grad_tok = jnp.dot(grad_values, w_value.T, preferred_element_type=jnp.float32).astype(jnp.bfloat16)
        grad_key = (values_bf.astype(jnp.float32) * grad_in).astype(jnp.bfloat16)
        grad_query = (gated_state * incoming).astype(jnp.bfloat16)
        part_filter = jnp.dot(cosines.T, fading * grad_kernel, precision=exact_mode) * kernel_scale
        part_bias = lax.optimization_barrier(jnp.sum(mixed_in * grad_state, axis=0))
        return (mixed_out, grad_tok, grad_key, grad_query, part_filter, part_bias)
    results = lax.map(per_stream, (tokens, gate_k, gate_q, cotangent))
    return (results[0], results[1], results[2], results[3], lax.optimization_barrier(jnp.sum(results[4], axis=0)), lax.optimization_barrier(jnp.sum(results[5], axis=0)))
```

```python
import math

import jax
import jax.numpy as jnp
import numpy as np
from jax import lax
from jax.sharding import PartitionSpec as P

BF = jnp.bfloat16
F32 = jnp.float32


def tables(block, order):
    pos = np.arange(block, dtype=np.float64)
    harm = 2.0 * np.pi / block * np.arange(1, order + 1, dtype=np.float64)
    half = np.pi / block * (2.0 * np.arange(block // 2, dtype=np.float64) + 1.0)
    even = harm[:, None] * pos[None, :]
    odd = half[:, None] * pos[None, :]
    dft = np.concatenate([np.cos(even), np.sin(even), np.cos(odd), np.sin(odd)])
    cross = np.sin(odd) @ np.cos(even).T
    return dft.astype(np.float32), cross.astype(np.float32)


def dot(a, b):
    return jnp.dot(a.astype(BF), b.astype(BF), preferred_element_type=F32)


def body(tokens, w_value, gate_k, gate_q, filter_weight, decay, skip_bias, cotangent):
    tok = tokens[0]
    block, width = tok.shape
    groups = lax.axis_size(("dp", "seq"))
    index = lax.axis_index(("dp", "seq"))
    length = block * groups
    order = filter_weight.shape[0]
    scale = 1.0 / math.sqrt(order * length)
    dft_np, cross_np = tables(block, order)
    dft = jnp.asarray(dft_np)
    cross = jnp.asarray(cross_np)
    n_even = 2 * order
    half = block // 2
    values = jnp.dot(
        lax.all_gather(tok, "chan", axis=1, tiled=True), w_value, preferred_element_type=F32
    ).astype(BF).astype(F32)
    key = gate_k[0].astype(F32)
    query = gate_q[0].astype(F32)
    inc = cotangent[0].astype(F32)
    mixed_in = key * values
    grad_state = query * inc
    pos = jnp.arange(block, dtype=F32)[:, None] / length
    fade = jnp.exp(-pos * decay[None, :])
    grow = jnp.exp(pos * decay[None, :])
    x_spec = dot(dft, mixed_in * grow)
    g_spec = dot(dft, grad_state * fade)
    weights = filter_weight * scale
    kern_c = jnp.sum(weights, axis=0, keepdims=True)
    kern_s = jnp.dot(cross, weights, precision=lax.Precision.HIGHEST)

    states = jnp.concatenate([x_spec[:n_even], g_spec[:n_even]])
    sub = width // groups
    mine = lax.all_to_all(
        states.reshape(2 * n_even, groups, sub), ("dp", "seq"), split_axis=1, concat_axis=1, tiled=True
    )
    dec = lax.dynamic_slice_in_dim(decay, index * sub, sub, 0)
    ids = jnp.arange(groups)
    gap = (ids[:, None] - ids[None, :]).astype(F32)
    low = jnp.where(
        gap[:, :, None] > 0, jnp.exp(-jnp.maximum(gap, 0.0)[:, :, None] * dec * (block / length)), 0.0
    )
    carried_x = jnp.einsum("ijc,rjc->ric", low, mine[:n_even], precision=lax.Precision.HIGHEST)
    carried_g = jnp.einsum("jic,rjc->ric", low, mine[n_even:], precision=lax.Precision.HIGHEST)
    back = lax.all_to_all(
        jnp.concatenate([carried_x, carried_g]), ("dp", "seq"), split_axis=1, concat_axis=1, tiled=True
    ).reshape(2 * n_even, width)
    z_x, z_g = back[:n_even], back[n_even:]

    two = jnp.concatenate([weights, weights])
    xe, ge = x_spec[:n_even], g_spec[:n_even]
    xc, xs = x_spec[n_even : n_even + half], x_spec[n_even + half :]
    gc, gs = g_spec[n_even : n_even + half], g_spec[n_even + half :]
    inv = 1.0 / block
    y_spec = jnp.concatenate(
        [two * (z_x + 0.5 * xe), inv * (kern_c * xc - kern_s * xs), inv * (kern_c * xs + kern_s * xc)]
    )
    p_spec = jnp.concatenate(
        [two * (z_g + 0.5 * ge), inv * (kern_c * gc + kern_s * gs), inv * (kern_c * gs - kern_s * gc)]
    )
    gated_state = fade * dot(dft.T, y_spec) + skip_bias * mixed_in
    grad_in = grow * dot(dft.T, p_spec) + skip_bias * grad_state

    n_c = gc * xc + gs * xs
    n_s = gs * xc - gc * xs
    prod = ge * (z_x + 0.5 * xe)
    part = scale * (
        prod[:order]
        + prod[order:]
        + inv * (jnp.sum(n_c, axis=0, keepdims=True) + jnp.dot(cross.T, n_s, precision=lax.Precision.HIGHEST))
    )
    part_bias = jnp.sum(mixed_in * grad_state, axis=0, keepdims=True)
    sums = lax.psum(jnp.concatenate([part, part_bias]), ("dp", "seq"))

    mixed = (query * gated_state).astype(BF)
    grad_values = (key * grad_in).astype(BF)
    terms = lax.dot_general(
        grad_values, w_value, (((1,), (1,)), ((), ())), preferred_element_type=F32
    )
    grad_tok = lax.psum_scatter(terms, "chan", scatter_dimension=1, tiled=True).astype(BF)
    grad_key = (values * grad_in).astype(BF)
    grad_query = (gated_state * inc).astype(BF)
    return (
        mixed[None],
        grad_tok[None],
        grad_key[None],
        grad_query[None],
        sums[:order],
        sums[order],
    )


def solution(mesh):
    rows = P(None, ("dp", "seq"), "chan")
    cols = P(None, "chan")
    return jax.shard_map(
        body,
        mesh=mesh,
        in_specs=(rows, cols, rows, rows, cols, P("chan"), P("chan"), rows),
        out_specs=(rows, rows, rows, rows, cols, P("chan")),
        check_vma=False,
    )
```

```python
import functools
import math

import jax
import jax.numpy as jnp
import numpy as np
from jax import lax
from jax.experimental import pallas as pl
from jax.experimental.pallas import tpu as pltpu
from jax.sharding import PartitionSpec as P

BF = jnp.bfloat16
F32 = jnp.float32
MESH = pl.DeviceIdType.MESH
EXACT = lax.Precision.HIGHEST
NT = (((1,), (1,)), ((), ()))


def tables(block, order):
    pos = np.arange(block, dtype=np.float64)
    harm = 2.0 * np.pi / block * np.arange(1, order + 1, dtype=np.float64)
    half = np.pi / block * (2.0 * np.arange(block // 2, dtype=np.float64) + 1.0)
    even = harm[:, None] * pos[None, :]
    odd = half[:, None] * pos[None, :]
    pair = np.stack([np.cos(even).reshape(-1, 8, block), np.sin(even).reshape(-1, 8, block)], 1)
    dft = np.concatenate([pair.reshape(2 * order, block), np.cos(odd), np.sin(odd)])
    cross = np.sin(odd) @ np.cos(even).T
    return dft.astype(np.float32), cross.astype(np.float32)


def mm(a, b):
    return jnp.dot(a, b, preferred_element_type=F32)


def kernel(
    seq_size, length,
    tok_h, w_h, gk_h, gq_h, fw_h, cot_h, dft_h, idft_h, cross_h, crosst_h, dec, bias,
    mixed_o, gtok_o, gkey_o, gqry_o, gf_o, gb_o,
    tok, w, gk, gq, fw, cot, dft, idft, cross, crosst,
    fade, grow, gs, gin, xin, val, gval, acc, gspec, xspec, pspec, kern, wts, carry,
    src, dst, terms, send_a, send_p, send_s, send_z, got_a, got_b, got_z,
    load_sem, ag_send, ag_recv, rs_send, rs_recv, st_send, st_recv,
):
    block, width = gk.shape
    rows = block // 2
    order = fw.shape[0]
    groups = 2 * seq_size
    n_even = 2 * order
    half = block // 2
    lanes = src.shape[3]
    n_rg = n_even // 16
    n_cg = width // lanes
    scale = 1.0 / math.sqrt(order * length)
    inv = 1.0 / block

    dp, seq, chan = lax.axis_index("dp"), lax.axis_index("seq"), lax.axis_index("chan")
    me = dp * seq_size + seq
    y, zh = chan // 2, chan % 2

    def chan_at(dy, other):
        return ((y + dy) % 4) * 2 + (zh + other) % 2

    def at_chan(c):
        return (dp, seq, c)

    up, down, across = at_chan(chan_at(1, 0)), at_chan(chan_at(3, 0)), at_chan(chan_at(0, 1))

    def peer(i):
        b = (me + i) % groups
        return b, (b // seq_size, b % seq_size, chan)

    loads = {}
    order_of = [
        ("gq", gq_h, gq), ("cot", cot_h, cot), ("dft", dft_h, dft), ("fw", fw_h, fw), ("cross", cross_h, cross),
        ("gk", gk_h, gk), ("idft", idft_h, idft), ("crosst", crosst_h, crosst), ("w", w_h, w),
        ("tok", tok_h, tok.at[chan]),
    ]
    for i, (name, a, b) in enumerate(order_of):
        loads[name] = pltpu.make_async_copy(a, b, load_sem.at[i])
        loads[name].start()

    barrier = pltpu.get_barrier_semaphore()
    for target in (up, down, across):
        pl.semaphore_signal(barrier, inc=1, device_id=target, device_id_type=MESH)

    def greet(i, carry_):
        pl.semaphore_signal(barrier, inc=1, device_id=peer(i)[1], device_id_type=MESH)
        return carry_

    lax.fori_loop(1, groups, greet, 0)
    pl.semaphore_wait(barrier, groups + 2)

    top, bot = pl.ds(0, rows), pl.ds(rows, rows)

    ag = []

    def gather(i, slot, part, target, first=False):
        s = tok_h.at[part] if first else tok.at[slot, part]
        cp = pltpu.make_async_remote_copy(
            src_ref=s, dst_ref=tok.at[slot, part], send_sem=ag_send.at[i], recv_sem=ag_recv.at[i],
            device_id=target, device_id_type=MESH,
        )
        cp.start()
        ag.append(cp)

    def arrived(i, slot, part):
        r = tok.at[slot, part]
        pltpu.make_async_copy(r, r, ag_recv.at[i]).wait()

    gather(0, chan, top, across, True)
    gather(2, chan, top, up, True)
    gather(4, chan, bot, down, True)
    gather(1, chan, bot, across, True)
    gather(3, chan, bot, up, True)
    gather(5, chan, top, down, True)

    def spread(trip, single=False):
        def one(i, carry_):
            b, target = peer(i)
            s = src.at[trip, 0] if single else src.at[trip, b]
            pltpu.make_async_remote_copy(
                src_ref=s, dst_ref=dst.at[trip, me], send_sem=st_send.at[trip], recv_sem=st_recv.at[trip],
                device_id=target, device_id_type=MESH,
            ).start()
            return carry_

        lax.fori_loop(1, groups, one, 0, unroll=True)
        dst[trip, me] = src[trip, 0] if single else src[trip, me]

    def landed(trip):
        r = dst.at[trip, pl.ds(0, groups - 1)]
        pltpu.make_async_copy(r, r, st_recv.at[trip]).wait()

    def left(trip):
        r = src.at[trip, pl.ds(0, groups - 1)]
        pltpu.make_async_copy(r, r, st_send.at[trip]).wait()

    def stage(trip, ref):
        for rg in range(n_rg):
            for cg in range(n_cg):
                src[trip, rg * n_cg + cg] = ref[pl.ds(16 * rg, 16), pl.ds(lanes * cg, lanes)].astype(BF)

    def unstage(trip):
        for rg in range(n_rg):
            for cg in range(n_cg):
                carry[pl.ds(16 * rg, 16), pl.ds(lanes * cg, lanes)] = dst[trip, rg * n_cg + cg].astype(F32)

    loads["gq"].wait()
    loads["cot"].wait()
    pos = lax.broadcasted_iota(jnp.int32, (block, width), 0).astype(F32) * (1.0 / length)
    rate = pos * dec[...]
    fade[...] = jnp.exp(-rate)
    grow[...] = jnp.exp(rate)
    gs[...] = gq[...].astype(F32) * cot[...].astype(F32)
    loads["dft"].wait()
    gspec[...] = mm(dft[...], (gs[...] * fade[...]).astype(BF))
    stage(0, gspec)
    spread(0)

    loads["fw"].wait()
    loads["cross"].wait()
    scaled = fw[...] * scale
    for rg in range(n_rg):
        eight = scaled[8 * rg : 8 * rg + 8]
        wts[pl.ds(16 * rg, 8), :] = eight
        wts[pl.ds(16 * rg + 8, 8), :] = eight
    kern[...] = jnp.dot(cross[...], scaled, precision=EXACT, preferred_element_type=F32)
    kern_c = jnp.sum(scaled, axis=0, keepdims=True)

    c_up, c_down, c_far = chan_at(1, 0), chan_at(3, 0), chan_at(2, 0)
    o_me, o_up, o_down, o_far = chan_at(0, 1), chan_at(1, 1), chan_at(3, 1), chan_at(2, 1)
    arrived(2, c_down, top)
    gather(6, c_down, top, up)
    arrived(4, c_up, bot)
    gather(7, c_up, bot, down)

    col0 = pl.multiple_of((me % n_cg) * lanes, lanes)
    rho = jnp.exp(dec[:, pl.ds(col0, lanes)] * (-block / length))
    landed(0)

    def back(i, r):
        b = groups - 1 - i
        src[1, b] = r.astype(BF)
        return rho * (r + dst[0, b].astype(F32))

    lax.fori_loop(0, groups, back, jnp.zeros((16, lanes), F32), unroll=4)
    spread(1)

    arrived(0, o_me, top)
    gather(8, o_me, top, up)
    gather(11, o_me, top, down)

    loads["gk"].wait()
    loads["idft"].wait()
    landed(1)
    unstage(1)
    pspec[pl.ds(0, n_even), :] = (wts[...] * (carry[...] + 0.5 * gspec[pl.ds(0, n_even), :])).astype(BF)
    gc, gsn = gspec[pl.ds(n_even, half), :], gspec[pl.ds(n_even + half, half), :]
    pspec[pl.ds(n_even, half), :] = (inv * (kern_c * gc + kern[...] * gsn)).astype(BF)
    pspec[pl.ds(n_even + half, half), :] = (inv * (kern_c * gsn - kern[...] * gc)).astype(BF)
    gin[...] = grow[...] * mm(idft[...], pspec[...]) + bias[...] * gs[...]
    gval[...] = (gk[...].astype(F32) * gin[...]).astype(BF)

    arrived(1, o_me, bot)
    gather(10, o_me, bot, down)
    gather(9, o_me, bot, up)

    loads["w"].wait()
    loads["tok"].wait()

    def w_of(c):
        return w[pl.ds(pl.multiple_of(c * width, width), width), :]

    acc[...] = mm(tok[chan], w_of(chan))
    arrived(3, c_down, bot)
    acc[...] += mm(tok[c_down], w_of(c_down))
    arrived(5, c_up, top)
    acc[...] += mm(tok[c_up], w_of(c_up))
    acc[...] += mm(tok[o_me], w_of(o_me))

    arrived(8, o_down, top)
    gather(12, o_down, top, up)
    arrived(10, o_up, bot)
    gather(13, o_up, bot, down)

    rs = []

    def reduce_send(i, s, d, target):
        cp = pltpu.make_async_remote_copy(
            src_ref=s, dst_ref=d, send_sem=rs_send.at[i], recv_sem=rs_recv.at[i], device_id=target, device_id_type=MESH,
        )
        cp.start()
        rs.append(cp)

    def reduce_wait(i, r):
        pltpu.make_async_copy(r, r, rs_recv.at[i]).wait()

    def term(p, dy):
        terms[4 * p + dy] = lax.dot_general(gval[...], w_of(chan_at(dy, 1 - p)), NT, preferred_element_type=F32)

    def phase_start(p):
        term(p, 2)
        send_a[p, 0] = terms[4 * p + 2, top].astype(BF)
        send_a[p, 1] = terms[4 * p + 2, bot].astype(BF)
        reduce_send(6 * p, send_a.at[p, 0], got_a.at[p, 0], up)
        reduce_send(6 * p + 1, send_a.at[p, 1], got_a.at[p, 1], down)
        term(p, 1)
        send_p[p, 0] = terms[4 * p + 1, bot].astype(BF)
        reduce_send(6 * p + 2, send_p.at[p, 0], got_b.at[p, 0, bot], up)
        term(p, 3)
        send_p[p, 1] = terms[4 * p + 3, top].astype(BF)
        reduce_send(6 * p + 3, send_p.at[p, 1], got_b.at[p, 1, top], down)

    def phase_middle(p):
        reduce_wait(6 * p, got_a.at[p, 0])
        send_s[p, 0] = (terms[4 * p + 1, top] + got_a[p, 0].astype(F32)).astype(BF)
        reduce_send(6 * p + 4, send_s.at[p, 0], got_b.at[p, 0, top], up)
        reduce_wait(6 * p + 1, got_a.at[p, 1])
        send_s[p, 1] = (terms[4 * p + 3, bot] + got_a[p, 1].astype(F32)).astype(BF)
        reduce_send(6 * p + 5, send_s.at[p, 1], got_b.at[p, 1, bot], down)

    def phase_end(p):
        reduce_wait(6 * p + 2, got_b.at[p, 0, bot])
        reduce_wait(6 * p + 3, got_b.at[p, 1, top])
        reduce_wait(6 * p + 4, got_b.at[p, 0, top])
        reduce_wait(6 * p + 5, got_b.at[p, 1, bot])
        return terms[4 * p] + got_b[p, 0].astype(F32) + got_b[p, 1].astype(F32)

    phase_start(0)

    arrived(6, c_far, top)
    arrived(7, c_far, bot)
    acc[...] += mm(tok[c_far], w_of(c_far))
    arrived(9, o_down, bot)
    acc[...] += mm(tok[o_down], w_of(o_down))
    arrived(11, o_up, top)
    acc[...] += mm(tok[o_up], w_of(o_up))
    arrived(12, o_far, top)
    arrived(13, o_far, bot)
    val[...] = (acc[...] + mm(tok[o_far], w_of(o_far))).astype(BF)
    xin[...] = gk[...].astype(F32) * val[...].astype(F32)
    xspec[...] = mm(dft[...], (xin[...] * grow[...]).astype(BF))
    stage(2, xspec)
    spread(2)

    xc, xs = xspec[pl.ds(n_even, half), :], xspec[pl.ds(n_even + half, half), :]
    gc, gsn = gspec[pl.ds(n_even, half), :], gspec[pl.ds(n_even + half, half), :]
    loads["crosst"].wait()
    part = inv * (
        jnp.sum(gc * xc + gsn * xs, axis=0, keepdims=True)
        + jnp.dot(crosst[...], gsn * xc - gc * xs, precision=EXACT, preferred_element_type=F32)
    )
    part_b = jnp.broadcast_to(jnp.sum(xin[...] * gs[...], axis=0, keepdims=True), (8, width))
    for rg in range(n_rg):
        both = jnp.concatenate([part[8 * rg : 8 * rg + 8], part_b]).astype(BF)
        for cg in range(n_cg):
            src[3, rg * n_cg + cg] = both[:, lanes * cg : lanes * cg + lanes]
    spread(3)

    phase_middle(0)
    phase_start(1)
    term(0, 0)

    landed(2)
    landed(3)

    def fore(b, state):
        z, g_sum, b_sum = state
        x_b, g_b, p_b = dst[2, b].astype(F32), dst[0, b].astype(F32), dst[3, b].astype(F32)
        src[4, b] = z.astype(BF)
        prod = g_b * (z + 0.5 * x_b)
        return rho * (z + x_b), g_sum + prod[0:8] + prod[8:16] + p_b[0:8], b_sum + p_b[8:16]

    eight0 = jnp.zeros((8, lanes), F32)
    _, g_sum, b_sum = lax.fori_loop(0, groups, fore, (jnp.zeros((16, lanes), F32), eight0, eight0), unroll=4)
    spread(4)
    src[5, 0] = jnp.concatenate([g_sum * scale, b_sum]).astype(BF)
    spread(5, True)

    phase_middle(1)
    term(1, 0)
    send_z[...] = phase_end(0).astype(BF)
    reduce_send(12, send_z, got_z, across)

    landed(4)
    unstage(4)
    pspec[pl.ds(0, n_even), :] = (wts[...] * (carry[...] + 0.5 * xspec[pl.ds(0, n_even), :])).astype(BF)
    pspec[pl.ds(n_even, half), :] = (inv * (kern_c * xc - kern[...] * xs)).astype(BF)
    pspec[pl.ds(n_even + half, half), :] = (inv * (kern_c * xs + kern[...] * xc)).astype(BF)
    state = fade[...] * mm(idft[...], pspec[...]) + bias[...] * xin[...]
    mixed_o[...] = (gq[...].astype(F32) * state).astype(BF)
    gqry_o[...] = (cot[...].astype(F32) * state).astype(BF)
    gkey_o[...] = (val[...].astype(F32) * gin[...]).astype(BF)

    acc[...] = phase_end(1)

    landed(5)
    for rg in range(n_rg):
        for cg in range(n_cg):
            d = dst[5, rg * n_cg + cg].astype(F32)
            gf_o[pl.ds(8 * rg, 8), pl.ds(lanes * cg, lanes)] = d[0:8]
            if rg == 0:
                gb_o[:, pl.ds(lanes * cg, lanes)] = d[8:9]

    reduce_wait(12, got_z)
    gtok_o[...] = (acc[...] + got_z[...].astype(F32)).astype(BF)

    for trip in range(6):
        left(trip)
    for cp in ag:
        cp.wait_send()
    for cp in rs:
        cp.wait_send()


def body(tokens, w_value, gate_k, gate_q, filter_weight, decay, skip_bias, cotangent):
    _, block, width = tokens.shape
    seq_size = lax.axis_size("seq")
    groups = seq_size * lax.axis_size("dp")
    chans = lax.axis_size("chan")
    order = filter_weight.shape[0]
    length = block * groups
    half = block // 2
    n_even = 2 * order
    n_spec = n_even + block
    lanes = width * (n_even // 16) // groups
    dft, cross = tables(block, order)
    any_spec = pl.BlockSpec(memory_space=pl.ANY)
    vmem = pl.BlockSpec(memory_space=pltpu.VMEM)
    wide = (block, width)
    outs = pl.pallas_call(
        functools.partial(kernel, seq_size, length),
        out_shape=[jax.ShapeDtypeStruct(wide, BF)] * 4
        + [jax.ShapeDtypeStruct((order, width), F32), jax.ShapeDtypeStruct((1, width), F32)],
        in_specs=[any_spec] * 10 + [vmem] * 2,
        out_specs=[vmem] * 6,
        scratch_shapes=[
            pltpu.VMEM((chans, block, width), BF),
            pltpu.VMEM(w_value.shape, BF),
            pltpu.VMEM(wide, BF),
            pltpu.VMEM(wide, BF),
            pltpu.VMEM((order, width), F32),
            pltpu.VMEM(wide, BF),
            pltpu.VMEM((n_spec, block), BF),
            pltpu.VMEM((block, n_spec), BF),
            pltpu.VMEM((half, order), F32),
            pltpu.VMEM((order, half), F32),
            pltpu.VMEM(wide, F32),
            pltpu.VMEM(wide, F32),
            pltpu.VMEM(wide, F32),
            pltpu.VMEM(wide, F32),
            pltpu.VMEM(wide, F32),
            pltpu.VMEM(wide, BF),
            pltpu.VMEM(wide, BF),
            pltpu.VMEM(wide, F32),
            pltpu.VMEM((n_spec, width), F32),
            pltpu.VMEM((n_spec, width), F32),
            pltpu.VMEM((n_spec, width), BF),
            pltpu.VMEM((half, width), F32),
            pltpu.VMEM((n_even, width), F32),
            pltpu.VMEM((n_even, width), F32),
            pltpu.VMEM((6, groups, 16, lanes), BF),
            pltpu.VMEM((6, groups, 16, lanes), BF),
            pltpu.VMEM((8, block, width), F32),
            pltpu.VMEM((2, 2, block // 2, width), BF),
            pltpu.VMEM((2, 2, block // 2, width), BF),
            pltpu.VMEM((2, 2, block // 2, width), BF),
            pltpu.VMEM(wide, BF),
            pltpu.VMEM((2, 2, block // 2, width), BF),
            pltpu.VMEM((2, 2, block, width), BF),
            pltpu.VMEM(wide, BF),
            pltpu.SemaphoreType.DMA((10,)),
            pltpu.SemaphoreType.DMA((14,)),
            pltpu.SemaphoreType.DMA((14,)),
            pltpu.SemaphoreType.DMA((13,)),
            pltpu.SemaphoreType.DMA((13,)),
            pltpu.SemaphoreType.DMA((6,)),
            pltpu.SemaphoreType.DMA((6,)),
        ],
        compiler_params=pltpu.CompilerParams(
            collective_id=0, has_side_effects=True, vmem_limit_bytes=48 * 2**20
        ),
        name="hyena",
    )(
        tokens[0], w_value, gate_k[0], gate_q[0], filter_weight, cotangent[0],
        jnp.asarray(dft, BF), jnp.asarray(dft.T, BF), jnp.asarray(cross), jnp.asarray(cross.T),
        decay[None], skip_bias[None],
    )
    mixed, gtok, gkey, gqry, gfil, gbias = outs
    return mixed[None], gtok[None], gkey[None], gqry[None], gfil, gbias[0]


def solution(mesh):
    rows = P(None, ("dp", "seq"), "chan")
    cols = P(None, "chan")
    return jax.shard_map(
        body,
        mesh=mesh,
        in_specs=(rows, cols, rows, rows, cols, P("chan"), P("chan"), rows),
        out_specs=(rows, rows, rows, rows, cols, P("chan")),
        check_vma=False,
    )
```

```python
import functools
import math

import jax
import jax.numpy as jnp
import numpy as np
from jax import lax
from jax.experimental import pallas as pl
from jax.experimental.pallas import tpu as pltpu
from jax.sharding import PartitionSpec as P

BF = jnp.bfloat16
F32 = jnp.float32
MESH = pl.DeviceIdType.MESH
EXACT = lax.Precision.HIGHEST
NT = (((1,), (1,)), ((), ()))


def tables(block, order):
    pos = np.arange(block, dtype=np.float64)
    harm = 2.0 * np.pi / block * np.arange(1, order + 1, dtype=np.float64)
    half = np.pi / block * (2.0 * np.arange(block // 2, dtype=np.float64) + 1.0)
    even = harm[:, None] * pos[None, :]
    odd = half[:, None] * pos[None, :]
    pair = np.stack([np.cos(even).reshape(-1, 8, block), np.sin(even).reshape(-1, 8, block)], 1)
    dft = np.concatenate([pair.reshape(2 * order, block), np.cos(odd), np.sin(odd)])
    cross = np.sin(odd) @ np.cos(even).T
    return dft.astype(np.float32), cross.astype(np.float32)


def mm(a, b):
    return jnp.dot(a, b, preferred_element_type=F32)


def kernel(
    seq_size, length,
    tok_h, w_h, gk_h, gq_h, fw_h, cot_h, dft_h, idft_h, cross_h, crosst_h, dec_h, bias_h,
    mixed_o, gtok_o, gkey_o, gqry_o, gf_o, gb_o,
    tok, w, gk, gq, fw, cot, dft, idft, cross, crosst, dec, bias,
    fade, grow, gs, gin, xin, val, gval, acc, gspec, xspec, pspec, kern, wts, carry,
    src, dst, terms, send_a, send_p, send_s, send_z, got_a, got_b, got_z,
    load_sem, ag_send, ag_recv, rs_send, rs_recv, st_send, st_recv,
):
    block, width = gk.shape
    rows = block // 2
    order = fw.shape[0]
    groups = 2 * seq_size
    n_even = 2 * order
    half = block // 2
    lanes = src.shape[3]
    n_rg = n_even // 16
    n_cg = width // lanes
    scale = 1.0 / math.sqrt(order * length)
    inv = 1.0 / block

    dp, seq, chan = lax.axis_index("dp"), lax.axis_index("seq"), lax.axis_index("chan")
    me = dp * seq_size + seq
    y, zh = chan // 2, chan % 2

    def chan_at(dy, other):
        return ((y + dy) % 4) * 2 + (zh + other) % 2

    def at_chan(c):
        return (dp, seq, c)

    up, down, across = at_chan(chan_at(1, 0)), at_chan(chan_at(3, 0)), at_chan(chan_at(0, 1))

    def peer(i):
        b = (me + i) % groups
        return b, (b // seq_size, b % seq_size, chan)

    loads = {}
    order_of = [
        ("gq", gq_h, gq), ("cot", cot_h, cot), ("dec", dec_h, dec), ("dft", dft_h, dft), ("fw", fw_h, fw), ("cross", cross_h, cross),
        ("gk", gk_h, gk), ("idft", idft_h, idft), ("crosst", crosst_h, crosst), ("w", w_h, w),
        ("tok", tok_h, tok.at[chan]), ("bias", bias_h, bias),
    ]
    for i, (name, a, b) in enumerate(order_of):
        loads[name] = pltpu.make_async_copy(a, b, load_sem.at[i])
        loads[name].start()

    barrier = pltpu.get_barrier_semaphore()
    for target in (up, down, across):
        pl.semaphore_signal(barrier, inc=1, device_id=target, device_id_type=MESH)

    def greet(i, carry_):
        pl.semaphore_signal(barrier, inc=1, device_id=peer(i)[1], device_id_type=MESH)
        return carry_

    lax.fori_loop(1, groups, greet, 0)
    pl.semaphore_wait(barrier, groups + 2)

    top, bot = pl.ds(0, rows), pl.ds(rows, rows)

    ag = {}

    def gather(i, slot, part, target, first=False):
        s = tok_h.at[part] if first else tok.at[slot, part]
        cp = pltpu.make_async_remote_copy(
            src_ref=s, dst_ref=tok.at[slot, part], send_sem=ag_send.at[i], recv_sem=ag_recv.at[i],
            device_id=target, device_id_type=MESH,
        )
        cp.start()
        ag[i] = cp

    def arrived(i, slot, part):
        r = tok.at[slot, part]
        pltpu.make_async_copy(r, r, ag_recv.at[i]).wait()

    def sent(i):
        ag.pop(i).wait_send()

    gather(0, chan, top, across, True)
    gather(2, chan, top, up, True)
    gather(4, chan, bot, down, True)

    def spread(trip, single=False):
        def one(i, carry_):
            b, target = peer(i)
            s = src.at[trip, 0] if single else src.at[trip, b]
            pltpu.make_async_remote_copy(
                src_ref=s, dst_ref=dst.at[trip, me], send_sem=st_send.at[trip], recv_sem=st_recv.at[trip],
                device_id=target, device_id_type=MESH,
            ).start()
            return carry_

        lax.fori_loop(1, groups, one, 0, unroll=True)
        dst[trip, me] = src[trip, 0] if single else src[trip, me]

    def landed(trip):
        r = dst.at[trip, pl.ds(0, groups - 1)]
        pltpu.make_async_copy(r, r, st_recv.at[trip]).wait()

    def left(trip):
        r = src.at[trip, pl.ds(0, groups - 1)]
        pltpu.make_async_copy(r, r, st_send.at[trip]).wait()

    def stage(trip, ref):
        for rg in range(n_rg):
            for cg in range(n_cg):
                src[trip, rg * n_cg + cg] = ref[pl.ds(16 * rg, 16), pl.ds(lanes * cg, lanes)].astype(BF)

    def unstage(trip):
        for rg in range(n_rg):
            for cg in range(n_cg):
                carry[pl.ds(16 * rg, 16), pl.ds(lanes * cg, lanes)] = dst[trip, rg * n_cg + cg].astype(F32)

    loads["gq"].wait()
    loads["cot"].wait()
    loads["dec"].wait()
    pos = lax.broadcasted_iota(jnp.int32, (block, width), 0).astype(F32) * (1.0 / length)
    rate = pos * dec[...]
    fade[...] = jnp.exp(-rate)
    grow[...] = jnp.exp(rate)
    gs[...] = gq[...].astype(F32) * cot[...].astype(F32)
    loads["dft"].wait()
    gspec[...] = mm(dft[...], (gs[...] * fade[...]).astype(BF))
    stage(0, gspec)
    spread(0)

    c_up, c_down, c_far = chan_at(1, 0), chan_at(3, 0), chan_at(2, 0)
    o_me, o_up, o_down, o_far = chan_at(0, 1), chan_at(1, 1), chan_at(3, 1), chan_at(2, 1)
    sent(2)
    gather(3, chan, bot, up, True)
    sent(4)
    gather(5, chan, top, down, True)
    arrived(2, c_down, top)
    gather(6, c_down, top, up)
    arrived(4, c_up, bot)
    gather(7, c_up, bot, down)
    sent(0)
    gather(1, chan, bot, across, True)

    loads["fw"].wait()
    loads["cross"].wait()
    scaled = fw[...] * scale
    for rg in range(n_rg):
        eight = scaled[8 * rg : 8 * rg + 8]
        wts[pl.ds(16 * rg, 8), :] = eight
        wts[pl.ds(16 * rg + 8, 8), :] = eight
    kern[...] = jnp.dot(cross[...], scaled, precision=EXACT, preferred_element_type=F32)
    kern_c = jnp.sum(scaled, axis=0, keepdims=True)

    loads["w"].wait()
    loads["tok"].wait()

    def w_of(c):
        return w[pl.ds(pl.multiple_of(c * width, width), width), :]

    acc[...] = mm(tok[chan], w_of(chan))
    arrived(3, c_down, bot)
    acc[...] += mm(tok[c_down], w_of(c_down))
    arrived(5, c_up, top)
    acc[...] += mm(tok[c_up], w_of(c_up))
    arrived(0, o_me, top)
    gather(8, o_me, top, up)
    gather(11, o_me, top, down)

    col0 = pl.multiple_of((me % n_cg) * lanes, lanes)
    rho = jnp.exp(dec[:, pl.ds(col0, lanes)] * (-block / length))
    landed(0)

    def back(i, r):
        b = groups - 1 - i
        src[1, b] = r.astype(BF)
        return rho * (r + dst[0, b].astype(F32))

    lax.fori_loop(0, groups, back, jnp.zeros((16, lanes), F32), unroll=4)
    spread(1)

    arrived(8, o_down, top)
    gather(12, o_down, top, up)
    arrived(1, o_me, bot)
    gather(10, o_me, bot, down)
    gather(9, o_me, bot, up)

    loads["gk"].wait()
    loads["bias"].wait()
    loads["idft"].wait()
    landed(1)
    unstage(1)
    pspec[pl.ds(0, n_even), :] = (wts[...] * (carry[...] + 0.5 * gspec[pl.ds(0, n_even), :])).astype(BF)
    gc, gsn = gspec[pl.ds(n_even, half), :], gspec[pl.ds(n_even + half, half), :]
    pspec[pl.ds(n_even, half), :] = (inv * (kern_c * gc + kern[...] * gsn)).astype(BF)
    pspec[pl.ds(n_even + half, half), :] = (inv * (kern_c * gsn - kern[...] * gc)).astype(BF)
    gin[...] = grow[...] * mm(idft[...], pspec[...]) + bias[...] * gs[...]
    gval[...] = (gk[...].astype(F32) * gin[...]).astype(BF)

    rs = []

    def reduce_send(i, s, d, target):
        cp = pltpu.make_async_remote_copy(
            src_ref=s, dst_ref=d, send_sem=rs_send.at[i], recv_sem=rs_recv.at[i], device_id=target, device_id_type=MESH,
        )
        cp.start()
        rs.append(cp)

    def reduce_wait(i, r):
        pltpu.make_async_copy(r, r, rs_recv.at[i]).wait()

    def term(p, dy):
        terms[4 * p + dy] = lax.dot_general(gval[...], w_of(chan_at(dy, 1 - p)), NT, preferred_element_type=F32)

    def far_terms(p):
        term(p, 2)
        send_a[p, 0] = terms[4 * p + 2, top].astype(BF)
        send_a[p, 1] = terms[4 * p + 2, bot].astype(BF)
        reduce_send(6 * p, send_a.at[p, 0], got_a.at[p, 0], up)
        reduce_send(6 * p + 1, send_a.at[p, 1], got_a.at[p, 1], down)

    def near_terms(p):
        term(p, 1)
        send_p[p, 0] = terms[4 * p + 1, bot].astype(BF)
        reduce_send(6 * p + 2, send_p.at[p, 0], got_b.at[p, 0, bot], up)
        term(p, 3)
        send_p[p, 1] = terms[4 * p + 3, top].astype(BF)
        reduce_send(6 * p + 3, send_p.at[p, 1], got_b.at[p, 1, top], down)
        term(p, 0)

    def near_sums(p):
        reduce_wait(6 * p, got_a.at[p, 0])
        send_s[p, 0] = (terms[4 * p + 1, top] + got_a[p, 0].astype(F32)).astype(BF)
        reduce_send(6 * p + 4, send_s.at[p, 0], got_b.at[p, 0, top], up)
        reduce_wait(6 * p + 1, got_a.at[p, 1])
        send_s[p, 1] = (terms[4 * p + 3, bot] + got_a[p, 1].astype(F32)).astype(BF)
        reduce_send(6 * p + 5, send_s.at[p, 1], got_b.at[p, 1, bot], down)

    def own_sum(p):
        reduce_wait(6 * p + 2, got_b.at[p, 0, bot])
        reduce_wait(6 * p + 3, got_b.at[p, 1, top])
        reduce_wait(6 * p + 4, got_b.at[p, 0, top])
        reduce_wait(6 * p + 5, got_b.at[p, 1, bot])
        return terms[4 * p] + got_b[p, 0].astype(F32) + got_b[p, 1].astype(F32)

    arrived(10, o_up, bot)
    gather(13, o_up, bot, down)

    arrived(6, c_far, top)
    arrived(7, c_far, bot)
    acc[...] += mm(tok[c_far], w_of(c_far))
    acc[...] += mm(tok[o_me], w_of(o_me))
    arrived(9, o_down, bot)
    acc[...] += mm(tok[o_down], w_of(o_down))
    arrived(11, o_up, top)
    acc[...] += mm(tok[o_up], w_of(o_up))
    arrived(12, o_far, top)
    arrived(13, o_far, bot)
    val[...] = (acc[...] + mm(tok[o_far], w_of(o_far))).astype(BF)
    xin[...] = gk[...].astype(F32) * val[...].astype(F32)
    xspec[...] = mm(dft[...], (xin[...] * grow[...]).astype(BF))
    stage(2, xspec)
    spread(2)

    far_terms(0)
    near_terms(0)

    xc, xs = xspec[pl.ds(n_even, half), :], xspec[pl.ds(n_even + half, half), :]
    gc, gsn = gspec[pl.ds(n_even, half), :], gspec[pl.ds(n_even + half, half), :]
    loads["crosst"].wait()
    part = inv * (
        jnp.sum(gc * xc + gsn * xs, axis=0, keepdims=True)
        + jnp.dot(crosst[...], gsn * xc - gc * xs, precision=EXACT, preferred_element_type=F32)
    )
    part_b = jnp.broadcast_to(jnp.sum(xin[...] * gs[...], axis=0, keepdims=True), (8, width))
    for rg in range(n_rg):
        both = jnp.concatenate([part[8 * rg : 8 * rg + 8], part_b]).astype(BF)
        for cg in range(n_cg):
            src[3, rg * n_cg + cg] = both[:, lanes * cg : lanes * cg + lanes]
    spread(3)
    near_sums(0)
    far_terms(1)

    landed(2)

    def fore(b, state):
        z, g_sum = state
        x_b, g_b = dst[2, b].astype(F32), dst[0, b].astype(F32)
        src[4, b] = z.astype(BF)
        prod = g_b * (z + 0.5 * x_b)
        return rho * (z + x_b), g_sum + prod[0:8] + prod[8:16]

    zero = jnp.zeros((16, lanes), F32)
    _, g_sum = lax.fori_loop(0, groups, fore, (zero, jnp.zeros((8, lanes), F32)), unroll=4)
    spread(4)

    landed(3)
    p_sum = lax.fori_loop(0, groups, lambda b, t: t + dst[3, b].astype(F32), zero, unroll=4)
    src[5, 0] = jnp.concatenate([(g_sum + p_sum[0:8]) * scale, p_sum[8:16]]).astype(BF)
    spread(5, True)

    send_z[...] = own_sum(0).astype(BF)
    reduce_send(12, send_z, got_z, across)
    near_terms(1)
    near_sums(1)

    landed(4)
    unstage(4)
    pspec[pl.ds(0, n_even), :] = (wts[...] * (carry[...] + 0.5 * xspec[pl.ds(0, n_even), :])).astype(BF)
    pspec[pl.ds(n_even, half), :] = (inv * (kern_c * xc - kern[...] * xs)).astype(BF)
    pspec[pl.ds(n_even + half, half), :] = (inv * (kern_c * xs + kern[...] * xc)).astype(BF)
    state = fade[...] * mm(idft[...], pspec[...]) + bias[...] * xin[...]
    mixed_o[...] = (gq[...].astype(F32) * state).astype(BF)
    gqry_o[...] = (cot[...].astype(F32) * state).astype(BF)
    gkey_o[...] = (val[...].astype(F32) * gin[...]).astype(BF)

    acc[...] = own_sum(1)

    landed(5)
    for rg in range(n_rg):
        for cg in range(n_cg):
            d = dst[5, rg * n_cg + cg].astype(F32)
            gf_o[pl.ds(8 * rg, 8), pl.ds(lanes * cg, lanes)] = d[0:8]
            if rg == 0:
                gb_o[:, pl.ds(lanes * cg, lanes)] = d[8:9]

    reduce_wait(12, got_z)
    gtok_o[...] = (acc[...] + got_z[...].astype(F32)).astype(BF)

    for trip in range(6):
        left(trip)
    for cp in ag.values():
        cp.wait_send()
    for cp in rs:
        cp.wait_send()


def write_out(*refs):
    copies = [pltpu.make_async_copy(refs[i], refs[6 + i], refs[12].at[i]) for i in range(6)]
    for cp in copies:
        cp.start()
    for cp in copies:
        cp.wait()


def body(tokens, w_value, gate_k, gate_q, filter_weight, decay, skip_bias, cotangent):
    _, block, width = tokens.shape
    seq_size = lax.axis_size("seq")
    groups = seq_size * lax.axis_size("dp")
    chans = lax.axis_size("chan")
    order = filter_weight.shape[0]
    length = block * groups
    half = block // 2
    n_even = 2 * order
    n_spec = n_even + block
    lanes = width * (n_even // 16) // groups
    dft, cross = tables(block, order)
    hbm = pl.BlockSpec(memory_space=pltpu.HBM)
    vmem = pl.BlockSpec(memory_space=pltpu.VMEM)
    wide = (block, width)
    outs = pl.pallas_call(
        functools.partial(kernel, seq_size, length),
        out_shape=[jax.ShapeDtypeStruct(wide, BF)] * 4
        + [jax.ShapeDtypeStruct((order, width), F32), jax.ShapeDtypeStruct((1, width), F32)],
        in_specs=[hbm] * 12,
        out_specs=[vmem] * 6,
        scratch_shapes=[
            pltpu.VMEM((chans, block, width), BF),
            pltpu.VMEM(w_value.shape, BF),
            pltpu.VMEM(wide, BF),
            pltpu.VMEM(wide, BF),
            pltpu.VMEM((order, width), F32),
            pltpu.VMEM(wide, BF),
            pltpu.VMEM((n_spec, block), BF),
            pltpu.VMEM((block, n_spec), BF),
            pltpu.VMEM((half, order), F32),
            pltpu.VMEM((order, half), F32),
            pltpu.VMEM((1, width), F32),
            pltpu.VMEM((1, width), F32),
            pltpu.VMEM(wide, F32),
            pltpu.VMEM(wide, F32),
            pltpu.VMEM(wide, F32),
            pltpu.VMEM(wide, F32),
            pltpu.VMEM(wide, F32),
            pltpu.VMEM(wide, BF),
            pltpu.VMEM(wide, BF),
            pltpu.VMEM(wide, F32),
            pltpu.VMEM((n_spec, width), F32),
            pltpu.VMEM((n_spec, width), F32),
            pltpu.VMEM((n_spec, width), BF),
            pltpu.VMEM((half, width), F32),
            pltpu.VMEM((n_even, width), F32),
            pltpu.VMEM((n_even, width), F32),
            pltpu.VMEM((6, groups, 16, lanes), BF),
            pltpu.VMEM((6, groups, 16, lanes), BF),
            pltpu.VMEM((8, block, width), F32),
            pltpu.VMEM((2, 2, block // 2, width), BF),
            pltpu.VMEM((2, 2, block // 2, width), BF),
            pltpu.VMEM((2, 2, block // 2, width), BF),
            pltpu.VMEM(wide, BF),
            pltpu.VMEM((2, 2, block // 2, width), BF),
            pltpu.VMEM((2, 2, block, width), BF),
            pltpu.VMEM(wide, BF),
            pltpu.SemaphoreType.DMA((12,)),
            pltpu.SemaphoreType.DMA((14,)),
            pltpu.SemaphoreType.DMA((14,)),
            pltpu.SemaphoreType.DMA((13,)),
            pltpu.SemaphoreType.DMA((13,)),
            pltpu.SemaphoreType.DMA((6,)),
            pltpu.SemaphoreType.DMA((6,)),
        ],
        compiler_params=pltpu.CompilerParams(
            collective_id=0, has_side_effects=True, vmem_limit_bytes=60 * 2**20
        ),
        name="hyena",
    )(
        tokens[0], w_value, gate_k[0], gate_q[0], filter_weight, cotangent[0],
        jnp.asarray(dft, BF), jnp.asarray(dft.T, BF), jnp.asarray(cross), jnp.asarray(cross.T),
        decay[None], skip_bias[None],
    )
    mixed, gtok, gkey, gqry, gfil, gbias = pl.pallas_call(
        write_out,
        out_shape=[jax.ShapeDtypeStruct(o.shape, o.dtype) for o in outs],
        in_specs=[vmem] * 6,
        out_specs=[hbm] * 6,
        scratch_shapes=[pltpu.SemaphoreType.DMA((6,))],
        compiler_params=pltpu.CompilerParams(vmem_limit_bytes=60 * 2**20),
        name="write_out",
    )(*outs)
    return mixed[None], gtok[None], gkey[None], gqry[None], gfil, gbias[0]


def solution(mesh):
    rows = P(None, ("dp", "seq"), "chan")
    cols = P(None, "chan")
    return jax.shard_map(
        body,
        mesh=mesh,
        in_specs=(rows, cols, rows, rows, cols, P("chan"), P("chan"), rows),
        out_specs=(rows, rows, rows, rows, cols, P("chan")),
        check_vma=False,
    )
```

```python
import functools
import math

import jax
import jax.numpy as jnp
import numpy as np
from jax import lax
from jax.experimental import pallas as pl
from jax.experimental.pallas import tpu as pltpu
from jax.sharding import PartitionSpec as P

BF = jnp.bfloat16
F32 = jnp.float32
MESH = pl.DeviceIdType.MESH
EXACT = lax.Precision.HIGHEST
NT = (((1,), (1,)), ((), ()))


def tables(block, order):
    pos = np.arange(block, dtype=np.float64)
    harm = 2.0 * np.pi / block * np.arange(1, order + 1, dtype=np.float64)
    half = np.pi / block * (2.0 * np.arange(block // 2, dtype=np.float64) + 1.0)
    even = harm[:, None] * pos[None, :]
    odd = half[:, None] * pos[None, :]
    pair = np.stack([np.cos(even).reshape(-1, 8, block), np.sin(even).reshape(-1, 8, block)], 1)
    dft = np.concatenate([pair.reshape(2 * order, block), np.cos(odd), np.sin(odd)])
    cross = np.sin(odd) @ np.cos(even).T
    return dft.astype(np.float32), cross.astype(np.float32)


def mm(a, b):
    return jnp.dot(a, b, preferred_element_type=F32)


def kernel(
    seq_size, length,
    tok_h, w_h, gk_h, gq_h, fw_h, cot_h, dft_h, idft_h, cross_h, crosst_h, dec_h, bias_h,
    mixed_o, gtok_o, gkey_o, gqry_o, gf_o, gb_o,
    tok, w, gk, gq, fw, cot, dft, idft, cross, crosst, dec, bias,
    fade, grow, gs, gin, xin, val, gval, acc, gspec, xspec, pspec, kern, wts, carry,
    src, dst, terms, send_a, send_p, send_s, send_z, got_a, got_b, got_z,
    load_sem, ag_send, ag_recv, rs_send, rs_recv, st_send, st_recv, hop_send, hop_recv,
):
    block, width = gk.shape
    rows = block // 2
    order = fw.shape[0]
    groups = 2 * seq_size
    n_even = 2 * order
    half = block // 2
    lanes = src.shape[3]
    n_rg = n_even // 16
    n_cg = width // lanes
    scale = 1.0 / math.sqrt(order * length)
    inv = 1.0 / block

    dp, seq, chan = lax.axis_index("dp"), lax.axis_index("seq"), lax.axis_index("chan")
    me = dp * seq_size + seq
    y, zh = chan // 2, chan % 2

    def chan_at(dy, other):
        return ((y + dy) % 4) * 2 + (zh + other) % 2

    def at_chan(c):
        return (dp, seq, c)

    up, down, across = at_chan(chan_at(1, 0)), at_chan(chan_at(3, 0)), at_chan(chan_at(0, 1))

    def peer(i):
        b = (me + i) % groups
        return b, (b // seq_size, b % seq_size, chan)

    barrier = pltpu.get_barrier_semaphore()
    for target in (up, down, across):
        pl.semaphore_signal(barrier, inc=1, device_id=target, device_id_type=MESH)

    def greet(i, carry_):
        pl.semaphore_signal(barrier, inc=1, device_id=peer(i)[1], device_id_type=MESH)
        return carry_

    lax.fori_loop(1, groups, greet, 0)
    loads = {}
    order_of = [
        ("gq", gq_h, gq), ("cot", cot_h, cot), ("dec", dec_h, dec), ("dft", dft_h, dft), ("fw", fw_h, fw), ("cross", cross_h, cross),
        ("gk", gk_h, gk), ("idft", idft_h, idft), ("crosst", crosst_h, crosst), ("w", w_h, w),
        ("tok", tok_h, tok.at[chan]), ("bias", bias_h, bias),
    ]
    for i, (name, a, b) in enumerate(order_of):
        loads[name] = pltpu.make_async_copy(a, b, load_sem.at[i])
        loads[name].start()
    def stage(trip, ref):
        for rg in range(n_rg):
            for cg in range(n_cg):
                src[trip, rg * n_cg + cg] = ref[pl.ds(16 * rg, 16), pl.ds(lanes * cg, lanes)].astype(BF)

    pl.semaphore_wait(barrier, groups + 2)

    top, bot = pl.ds(0, rows), pl.ds(rows, rows)

    ag = {}

    def gather(i, slot, part, target, first=False):
        s = tok_h.at[part] if first else tok.at[slot, part]
        cp = pltpu.make_async_remote_copy(
            src_ref=s, dst_ref=tok.at[slot, part], send_sem=ag_send.at[i], recv_sem=ag_recv.at[i],
            device_id=target, device_id_type=MESH,
        )
        cp.start()
        ag[i] = cp

    def arrived(i, slot, part):
        r = tok.at[slot, part]
        pltpu.make_async_copy(r, r, ag_recv.at[i]).wait()

    def sent(i):
        ag.pop(i).wait_send()

    gather(0, chan, top, across, True)
    gather(2, chan, top, up, True)
    gather(4, chan, bot, down, True)

    def spread(trip):
        def one(i, carry_):
            b, target = peer(i)
            s = src.at[trip, b]
            pltpu.make_async_remote_copy(
                src_ref=s, dst_ref=dst.at[trip, me], send_sem=st_send.at[trip], recv_sem=st_recv.at[trip],
                device_id=target, device_id_type=MESH,
            ).start()
            return carry_

        lax.fori_loop(1, groups, one, 0, unroll=True)
        dst[trip, me] = src[trip, me]

    side = 4
    at_x, at_z = seq % side, seq // side

    def place(b):
        return (b // seq_size) * seq_size + (b % side) * side + (b % seq_size) // side

    def hop(step, s, d, target):
        pltpu.make_async_remote_copy(
            src_ref=s, dst_ref=d, send_sem=hop_send.at[step], recv_sem=hop_recv.at[step],
            device_id=target, device_id_type=MESH,
        ).start()

    def hop_wait(step, n):
        r = dst.at[5, pl.ds(0, n)]
        pltpu.make_async_copy(r, r, hop_recv.at[step]).wait()

    def hop_left(step, n):
        r = dst.at[5, pl.ds(0, n)]
        pltpu.make_async_copy(r, r, hop_send.at[step]).wait()

    def z_peer(i):
        return (dp, ((at_z + i) % side) * side + at_x, chan)

    def x_peer(i):
        return (dp, at_z * side + (at_x + i) % side, chan)

    core_peer = (1 - dp, seq, chan)

    def landed(trip):
        r = dst.at[trip, pl.ds(0, groups - 1)]
        pltpu.make_async_copy(r, r, st_recv.at[trip]).wait()

    def left(trip):
        r = src.at[trip, pl.ds(0, groups - 1)]
        pltpu.make_async_copy(r, r, st_send.at[trip]).wait()

    def unstage(trip):
        for rg in range(n_rg):
            for cg in range(n_cg):
                carry[pl.ds(16 * rg, 16), pl.ds(lanes * cg, lanes)] = dst[trip, rg * n_cg + cg].astype(F32)

    loads["gq"].wait()
    loads["cot"].wait()
    loads["dec"].wait()
    pos = lax.broadcasted_iota(jnp.int32, (block, width), 0).astype(F32) * (1.0 / length)
    rate = pos * dec[...]
    fade[...] = jnp.exp(-rate)
    grow[...] = jnp.exp(rate)
    gs[...] = gq[...].astype(F32) * cot[...].astype(F32)
    loads["dft"].wait()
    gspec[...] = mm(dft[...], (gs[...] * fade[...]).astype(BF))
    stage(0, gspec)
    spread(0)
    loads["fw"].wait()
    loads["cross"].wait()
    scaled = fw[...] * scale
    for rg in range(n_rg):
        eight = scaled[8 * rg : 8 * rg + 8]
        wts[pl.ds(16 * rg, 8), :] = eight
        wts[pl.ds(16 * rg + 8, 8), :] = eight
    kern[...] = jnp.dot(cross[...], scaled, precision=EXACT, preferred_element_type=F32)
    kern_c = jnp.sum(scaled, axis=0, keepdims=True)


    c_up, c_down, c_far = chan_at(1, 0), chan_at(3, 0), chan_at(2, 0)
    o_me, o_up, o_down, o_far = chan_at(0, 1), chan_at(1, 1), chan_at(3, 1), chan_at(2, 1)
    sent(2)
    gather(3, chan, bot, up, True)
    sent(4)
    gather(5, chan, top, down, True)
    arrived(2, c_down, top)
    gather(6, c_down, top, up)
    arrived(4, c_up, bot)
    gather(7, c_up, bot, down)
    sent(0)
    gather(1, chan, bot, across, True)

    loads["w"].wait()
    loads["tok"].wait()

    def w_of(c):
        return w[pl.ds(pl.multiple_of(c * width, width), width), :]

    acc[...] = mm(tok[chan], w_of(chan))
    arrived(3, c_down, bot)
    acc[...] += mm(tok[c_down], w_of(c_down))
    arrived(5, c_up, top)
    acc[...] += mm(tok[c_up], w_of(c_up))
    arrived(0, o_me, top)
    gather(8, o_me, top, up)
    gather(11, o_me, top, down)

    loads["gk"].wait()
    loads["bias"].wait()
    loads["idft"].wait()
    arrived(8, o_down, top)
    gather(12, o_down, top, up)
    arrived(1, o_me, bot)
    gather(10, o_me, bot, down)
    gather(9, o_me, bot, up)

    col0 = pl.multiple_of((me % n_cg) * lanes, lanes)
    rho = jnp.exp(dec[:, pl.ds(col0, lanes)] * (-block / length))
    landed(0)

    def back(i, r):
        b = groups - 1 - i
        src[1, b] = r.astype(BF)
        return rho * (r + dst[0, b].astype(F32))

    lax.fori_loop(0, groups, back, jnp.zeros((16, lanes), F32), unroll=4)
    spread(1)

    arrived(10, o_up, bot)
    gather(13, o_up, bot, down)

    landed(1)
    unstage(1)
    pspec[pl.ds(0, n_even), :] = (wts[...] * (carry[...] + 0.5 * gspec[pl.ds(0, n_even), :])).astype(BF)
    gc, gsn = gspec[pl.ds(n_even, half), :], gspec[pl.ds(n_even + half, half), :]
    pspec[pl.ds(n_even, half), :] = (inv * (kern_c * gc + kern[...] * gsn)).astype(BF)
    pspec[pl.ds(n_even + half, half), :] = (inv * (kern_c * gsn - kern[...] * gc)).astype(BF)
    gin[...] = grow[...] * mm(idft[...], pspec[...]) + bias[...] * gs[...]
    gval[...] = (gk[...].astype(F32) * gin[...]).astype(BF)

    rs = []

    def reduce_send(i, s, d, target):
        cp = pltpu.make_async_remote_copy(
            src_ref=s, dst_ref=d, send_sem=rs_send.at[i], recv_sem=rs_recv.at[i], device_id=target, device_id_type=MESH,
        )
        cp.start()
        rs.append(cp)

    def reduce_wait(i, r):
        pltpu.make_async_copy(r, r, rs_recv.at[i]).wait()

    def term(p, dy):
        terms[4 * p + dy] = lax.dot_general(gval[...], w_of(chan_at(dy, 1 - p)), NT, preferred_element_type=F32)

    def far_terms(p):
        term(p, 2)
        send_a[p, 0] = terms[4 * p + 2, top].astype(BF)
        send_a[p, 1] = terms[4 * p + 2, bot].astype(BF)
        reduce_send(6 * p, send_a.at[p, 0], got_a.at[p, 0], up)
        reduce_send(6 * p + 1, send_a.at[p, 1], got_a.at[p, 1], down)

    def near_terms(p):
        term(p, 1)
        send_p[p, 0] = terms[4 * p + 1, bot].astype(BF)
        reduce_send(6 * p + 2, send_p.at[p, 0], got_b.at[p, 0, bot], up)
        term(p, 3)
        send_p[p, 1] = terms[4 * p + 3, top].astype(BF)
        reduce_send(6 * p + 3, send_p.at[p, 1], got_b.at[p, 1, top], down)
        term(p, 0)

    def near_sums(p):
        reduce_wait(6 * p, got_a.at[p, 0])
        send_s[p, 0] = (terms[4 * p + 1, top] + got_a[p, 0].astype(F32)).astype(BF)
        reduce_send(6 * p + 4, send_s.at[p, 0], got_b.at[p, 0, top], up)
        reduce_wait(6 * p + 1, got_a.at[p, 1])
        send_s[p, 1] = (terms[4 * p + 3, bot] + got_a[p, 1].astype(F32)).astype(BF)
        reduce_send(6 * p + 5, send_s.at[p, 1], got_b.at[p, 1, bot], down)

    def own_sum(p):
        reduce_wait(6 * p + 2, got_b.at[p, 0, bot])
        reduce_wait(6 * p + 3, got_b.at[p, 1, top])
        reduce_wait(6 * p + 4, got_b.at[p, 0, top])
        reduce_wait(6 * p + 5, got_b.at[p, 1, bot])
        return terms[4 * p] + got_b[p, 0].astype(F32) + got_b[p, 1].astype(F32)

    arrived(6, c_far, top)
    arrived(7, c_far, bot)
    acc[...] += mm(tok[c_far], w_of(c_far))
    acc[...] += mm(tok[o_me], w_of(o_me))
    arrived(9, o_down, bot)
    acc[...] += mm(tok[o_down], w_of(o_down))
    arrived(11, o_up, top)
    acc[...] += mm(tok[o_up], w_of(o_up))
    arrived(12, o_far, top)
    arrived(13, o_far, bot)
    val[...] = (acc[...] + mm(tok[o_far], w_of(o_far))).astype(BF)
    xin[...] = gk[...].astype(F32) * val[...].astype(F32)
    xspec[...] = mm(dft[...], (xin[...] * grow[...]).astype(BF))
    stage(2, xspec)
    spread(2)

    far_terms(0)
    near_terms(0)

    xc, xs = xspec[pl.ds(n_even, half), :], xspec[pl.ds(n_even + half, half), :]
    gc, gsn = gspec[pl.ds(n_even, half), :], gspec[pl.ds(n_even + half, half), :]
    loads["crosst"].wait()
    part = inv * (
        jnp.sum(gc * xc + gsn * xs, axis=0, keepdims=True)
        + jnp.dot(crosst[...], gsn * xc - gc * xs, precision=EXACT, preferred_element_type=F32)
    )
    part_b = jnp.broadcast_to(jnp.sum(xin[...] * gs[...], axis=0, keepdims=True), (8, width))
    for rg in range(n_rg):
        both = jnp.concatenate([part[8 * rg : 8 * rg + 8], part_b]).astype(BF)
        for cg in range(n_cg):
            src[3, rg * n_cg + cg] = both[:, lanes * cg : lanes * cg + lanes]
    spread(3)
    near_sums(0)
    far_terms(1)

    landed(2)

    def fore(b, state):
        z, g_sum = state
        x_b, g_b = dst[2, b].astype(F32), dst[0, b].astype(F32)
        src[4, b] = z.astype(BF)
        prod = g_b * (z + 0.5 * x_b)
        return rho * (z + x_b), g_sum + prod[0:8] + prod[8:16]

    zero = jnp.zeros((16, lanes), F32)
    _, g_sum = lax.fori_loop(0, groups, fore, (zero, jnp.zeros((8, lanes), F32)), unroll=4)
    spread(4)

    landed(3)
    p_sum = lax.fori_loop(0, groups, lambda b, t: t + dst[3, b].astype(F32), zero, unroll=4)
    src[5, 0] = jnp.concatenate([(g_sum + p_sum[0:8]) * scale, p_sum[8:16]]).astype(BF)
    dst[5, place(me)] = src[5, 0]
    for i in range(1, side):
        hop(0, src.at[5, 0], dst.at[5, place(me)], z_peer(i))

    send_z[...] = own_sum(0).astype(BF)
    reduce_send(12, send_z, got_z, across)
    near_terms(1)
    near_sums(1)

    hop_wait(0, side - 1)
    mine = pl.ds(dp * seq_size + at_x * side, side)
    for i in range(1, side):
        hop(1, dst.at[5, mine], dst.at[5, mine], x_peer(i))

    landed(4)
    unstage(4)
    pspec[pl.ds(0, n_even), :] = (wts[...] * (carry[...] + 0.5 * xspec[pl.ds(0, n_even), :])).astype(BF)
    pspec[pl.ds(n_even, half), :] = (inv * (kern_c * xc - kern[...] * xs)).astype(BF)
    pspec[pl.ds(n_even + half, half), :] = (inv * (kern_c * xs + kern[...] * xc)).astype(BF)
    state = fade[...] * mm(idft[...], pspec[...]) + bias[...] * xin[...]
    mixed_o[...] = (gq[...].astype(F32) * state).astype(BF)
    gqry_o[...] = (cot[...].astype(F32) * state).astype(BF)
    gkey_o[...] = (val[...].astype(F32) * gin[...]).astype(BF)

    acc[...] = own_sum(1)

    hop_wait(1, side * (side - 1))
    half_of = pl.ds(dp * seq_size, seq_size)
    hop(2, dst.at[5, half_of], dst.at[5, half_of], core_peer)
    hop_wait(2, seq_size)
    for rg in range(n_rg):
        for cg in range(n_cg):
            d = dst[5, place(rg * n_cg + cg)].astype(F32)
            gf_o[pl.ds(8 * rg, 8), pl.ds(lanes * cg, lanes)] = d[0:8]
            if rg == 0:
                gb_o[:, pl.ds(lanes * cg, lanes)] = d[8:9]
    reduce_wait(12, got_z)
    gtok_o[...] = (acc[...] + got_z[...].astype(F32)).astype(BF)

    for trip in range(5):
        left(trip)
    hop_left(0, side - 1)
    hop_left(1, side * (side - 1))
    hop_left(2, seq_size)
    for cp in ag.values():
        cp.wait_send()
    for cp in rs:
        cp.wait_send()


def write_out(*refs):
    copies = [pltpu.make_async_copy(refs[i], refs[6 + i], refs[12].at[i]) for i in range(6)]
    for cp in copies:
        cp.start()
    for cp in copies:
        cp.wait()


def body(tokens, w_value, gate_k, gate_q, filter_weight, decay, skip_bias, cotangent):
    _, block, width = tokens.shape
    seq_size = lax.axis_size("seq")
    groups = seq_size * lax.axis_size("dp")
    chans = lax.axis_size("chan")
    order = filter_weight.shape[0]
    length = block * groups
    half = block // 2
    n_even = 2 * order
    n_spec = n_even + block
    lanes = width * (n_even // 16) // groups
    dft, cross = tables(block, order)
    hbm = pl.BlockSpec(memory_space=pltpu.HBM)
    vmem = pl.BlockSpec(memory_space=pltpu.VMEM)
    wide = (block, width)
    outs = pl.pallas_call(
        functools.partial(kernel, seq_size, length),
        out_shape=[jax.ShapeDtypeStruct(wide, BF)] * 4
        + [jax.ShapeDtypeStruct((order, width), F32), jax.ShapeDtypeStruct((1, width), F32)],
        in_specs=[hbm] * 12,
        out_specs=[vmem] * 6,
        scratch_shapes=[
            pltpu.VMEM((chans, block, width), BF),
            pltpu.VMEM(w_value.shape, BF),
            pltpu.VMEM(wide, BF),
            pltpu.VMEM(wide, BF),
            pltpu.VMEM((order, width), F32),
            pltpu.VMEM(wide, BF),
            pltpu.VMEM((n_spec, block), BF),
            pltpu.VMEM((block, n_spec), BF),
            pltpu.VMEM((half, order), F32),
            pltpu.VMEM((order, half), F32),
            pltpu.VMEM((1, width), F32),
            pltpu.VMEM((1, width), F32),
            pltpu.VMEM(wide, F32),
            pltpu.VMEM(wide, F32),
            pltpu.VMEM(wide, F32),
            pltpu.VMEM(wide, F32),
            pltpu.VMEM(wide, F32),
            pltpu.VMEM(wide, BF),
            pltpu.VMEM(wide, BF),
            pltpu.VMEM(wide, F32),
            pltpu.VMEM((n_spec, width), F32),
            pltpu.VMEM((n_spec, width), F32),
            pltpu.VMEM((n_spec, width), BF),
            pltpu.VMEM((half, width), F32),
            pltpu.VMEM((n_even, width), F32),
            pltpu.VMEM((n_even, width), F32),
            pltpu.VMEM((6, groups, 16, lanes), BF),
            pltpu.VMEM((6, groups, 16, lanes), BF),
            pltpu.VMEM((8, block, width), F32),
            pltpu.VMEM((2, 2, block // 2, width), BF),
            pltpu.VMEM((2, 2, block // 2, width), BF),
            pltpu.VMEM((2, 2, block // 2, width), BF),
            pltpu.VMEM(wide, BF),
            pltpu.VMEM((2, 2, block // 2, width), BF),
            pltpu.VMEM((2, 2, block, width), BF),
            pltpu.VMEM(wide, BF),
            pltpu.SemaphoreType.DMA((12,)),
            pltpu.SemaphoreType.DMA((14,)),
            pltpu.SemaphoreType.DMA((14,)),
            pltpu.SemaphoreType.DMA((13,)),
            pltpu.SemaphoreType.DMA((13,)),
            pltpu.SemaphoreType.DMA((6,)),
            pltpu.SemaphoreType.DMA((6,)),
            pltpu.SemaphoreType.DMA((6,)),
            pltpu.SemaphoreType.DMA((6,)),
        ],
        compiler_params=pltpu.CompilerParams(
            collective_id=0, has_side_effects=True, vmem_limit_bytes=60 * 2**20
        ),
        name="hyena",
    )(
        tokens[0], w_value, gate_k[0], gate_q[0], filter_weight, cotangent[0],
        jnp.asarray(dft, BF), jnp.asarray(dft.T, BF), jnp.asarray(cross), jnp.asarray(cross.T),
        decay[None], skip_bias[None],
    )
    mixed, gtok, gkey, gqry, gfil, gbias = pl.pallas_call(
        write_out,
        out_shape=[jax.ShapeDtypeStruct(o.shape, o.dtype) for o in outs],
        in_specs=[vmem] * 6,
        out_specs=[hbm] * 6,
        scratch_shapes=[pltpu.SemaphoreType.DMA((6,))],
        compiler_params=pltpu.CompilerParams(vmem_limit_bytes=60 * 2**20),
        name="write_out",
    )(*outs)
    return mixed[None], gtok[None], gkey[None], gqry[None], gfil, gbias[0]


def solution(mesh):
    rows = P(None, ("dp", "seq"), "chan")
    cols = P(None, "chan")
    return jax.shard_map(
        body,
        mesh=mesh,
        in_specs=(rows, cols, rows, rows, cols, P("chan"), P("chan"), rows),
        out_specs=(rows, rows, rows, rows, cols, P("chan")),
        check_vma=False,
    )
```

```python
import functools
import math

import jax
import jax.numpy as jnp
import numpy as np
from jax import lax
from jax.experimental import pallas as pl
from jax.experimental.pallas import tpu as pltpu
from jax.sharding import PartitionSpec as P

BF = jnp.bfloat16
F32 = jnp.float32
MESH = pl.DeviceIdType.MESH
EXACT = lax.Precision.HIGHEST
NT = (((1,), (1,)), ((), ()))


def tables(block, order):
    pos = np.arange(block, dtype=np.float64)
    harm = 2.0 * np.pi / block * np.arange(1, order + 1, dtype=np.float64)
    half = np.pi / block * (2.0 * np.arange(block // 2, dtype=np.float64) + 1.0)
    even = harm[:, None] * pos[None, :]
    odd = half[:, None] * pos[None, :]
    pair = np.stack([np.cos(even).reshape(-1, 8, block), np.sin(even).reshape(-1, 8, block)], 1)
    dft = np.concatenate([pair.reshape(2 * order, block), np.cos(odd), np.sin(odd)])
    cross = np.sin(odd) @ np.cos(even).T
    return dft.astype(np.float32), cross.astype(np.float32)


def mm(a, b):
    return jnp.dot(a, b, preferred_element_type=F32)


def kernel(
    seq_size, length,
    tok_h, w_h, gk_h, gq_h, fw_h, cot_h, dft_h, idft_h, cross_h, crosst_h, dec_h, bias_h,
    mixed_o, gtok_o, gkey_o, gqry_o, gf_o, gb_o,
    tok, w, gk, gq, fw, cot, dft, idft, cross, crosst, dec, bias,
    fade, grow, gs, gin, xin, val, gval, acc, gspec, xspec, pspec, kern, wts, carry,
    src, dst, terms, send_a, send_p, send_s, send_z, got_a, got_b, got_z,
    load_sem, ag_send, ag_recv, rs_send, rs_recv, st_send, st_recv, hop_send, hop_recv,
):
    block, width = gk.shape
    rows = block // 2
    order = fw.shape[0]
    groups = 2 * seq_size
    n_even = 2 * order
    half = block // 2
    lanes = src.shape[3]
    n_rg = n_even // 16
    n_cg = width // lanes
    scale = 1.0 / math.sqrt(order * length)
    inv = 1.0 / block

    dp, seq, chan = lax.axis_index("dp"), lax.axis_index("seq"), lax.axis_index("chan")
    me = dp * seq_size + seq
    y, zh = chan // 2, chan % 2

    def chan_at(dy, other):
        return ((y + dy) % 4) * 2 + (zh + other) % 2

    def at_chan(c):
        return (dp, seq, c)

    up, down, across = at_chan(chan_at(1, 0)), at_chan(chan_at(3, 0)), at_chan(chan_at(0, 1))

    def peer(i):
        b = (me + i) % groups
        return b, (b // seq_size, b % seq_size, chan)

    barrier = pltpu.get_barrier_semaphore()
    for target in (up, down, across):
        pl.semaphore_signal(barrier, inc=1, device_id=target, device_id_type=MESH)

    def greet(i, carry_):
        pl.semaphore_signal(barrier, inc=1, device_id=peer(i)[1], device_id_type=MESH)
        return carry_

    lax.fori_loop(1, groups, greet, 0)
    loads = {}
    order_of = [
        ("gq", gq_h, gq), ("cot", cot_h, cot), ("dec", dec_h, dec), ("dft", dft_h, dft), ("fw", fw_h, fw), ("cross", cross_h, cross),
        ("gk", gk_h, gk), ("idft", idft_h, idft), ("crosst", crosst_h, crosst), ("w", w_h, w),
        ("tok", tok_h, tok.at[chan]), ("bias", bias_h, bias),
    ]
    for i, (name, a, b) in enumerate(order_of):
        loads[name] = pltpu.make_async_copy(a, b, load_sem.at[i])
        loads[name].start()
    def stage(trip, ref):
        for rg in range(n_rg):
            for cg in range(n_cg):
                src[trip, rg * n_cg + cg] = ref[pl.ds(16 * rg, 16), pl.ds(lanes * cg, lanes)].astype(BF)

    pl.semaphore_wait(barrier, groups + 2)

    top, bot = pl.ds(0, rows), pl.ds(rows, rows)

    ag = {}

    def gather(i, slot, part, target, first=False):
        s = tok_h.at[part] if first else tok.at[slot, part]
        cp = pltpu.make_async_remote_copy(
            src_ref=s, dst_ref=tok.at[slot, part], send_sem=ag_send.at[i], recv_sem=ag_recv.at[i],
            device_id=target, device_id_type=MESH,
        )
        cp.start()
        ag[i] = cp

    def arrived(i, slot, part):
        r = tok.at[slot, part]
        pltpu.make_async_copy(r, r, ag_recv.at[i]).wait()

    def sent(i):
        ag.pop(i).wait_send()

    gather(0, chan, top, across, True)
    gather(2, chan, top, up, True)
    gather(4, chan, bot, down, True)

    def spread(trip):
        def one(i, carry_):
            b, target = peer(i)
            s = src.at[trip, b]
            pltpu.make_async_remote_copy(
                src_ref=s, dst_ref=dst.at[trip, me], send_sem=st_send.at[trip], recv_sem=st_recv.at[trip],
                device_id=target, device_id_type=MESH,
            ).start()
            return carry_

        lax.fori_loop(1, groups, one, 0, unroll=True)
        dst[trip, me] = src[trip, me]

    side = 4
    at_x, at_z = seq % side, seq // side

    def place(b):
        return (b // seq_size) * seq_size + (b % side) * side + (b % seq_size) // side

    def hop(step, s, d, target):
        pltpu.make_async_remote_copy(
            src_ref=s, dst_ref=d, send_sem=hop_send.at[step], recv_sem=hop_recv.at[step],
            device_id=target, device_id_type=MESH,
        ).start()

    def hop_wait(step, n):
        r = dst.at[5, pl.ds(0, n)]
        pltpu.make_async_copy(r, r, hop_recv.at[step]).wait()

    def hop_left(step, n):
        r = dst.at[5, pl.ds(0, n)]
        pltpu.make_async_copy(r, r, hop_send.at[step]).wait()

    def z_peer(i):
        return (dp, ((at_z + i) % side) * side + at_x, chan)

    def x_peer(i):
        return (dp, at_z * side + (at_x + i) % side, chan)

    core_peer = (1 - dp, seq, chan)

    def landed(trip):
        r = dst.at[trip, pl.ds(0, groups - 1)]
        pltpu.make_async_copy(r, r, st_recv.at[trip]).wait()

    def left(trip):
        r = src.at[trip, pl.ds(0, groups - 1)]
        pltpu.make_async_copy(r, r, st_send.at[trip]).wait()

    def unstage(trip):
        for rg in range(n_rg):
            for cg in range(n_cg):
                carry[pl.ds(16 * rg, 16), pl.ds(lanes * cg, lanes)] = dst[trip, rg * n_cg + cg].astype(F32)

    loads["gq"].wait()
    loads["cot"].wait()
    loads["dec"].wait()
    pos = lax.broadcasted_iota(jnp.int32, (block, width), 0).astype(F32) * (1.0 / length)
    rate = pos * dec[...]
    fade[...] = jnp.exp(-rate)
    grow[...] = jnp.exp(rate)
    gs[...] = gq[...].astype(F32) * cot[...].astype(F32)
    loads["dft"].wait()
    gspec[...] = mm(dft[...], (gs[...] * fade[...]).astype(BF))
    stage(0, gspec)
    spread(0)
    loads["fw"].wait()
    loads["cross"].wait()
    scaled = fw[...] * scale
    for rg in range(n_rg):
        eight = scaled[8 * rg : 8 * rg + 8]
        wts[pl.ds(16 * rg, 8), :] = eight
        wts[pl.ds(16 * rg + 8, 8), :] = eight
    kern[...] = jnp.dot(cross[...], scaled, precision=EXACT, preferred_element_type=F32)
    kern_c = jnp.sum(scaled, axis=0, keepdims=True)


    c_up, c_down, c_far = chan_at(1, 0), chan_at(3, 0), chan_at(2, 0)
    o_me, o_up, o_down, o_far = chan_at(0, 1), chan_at(1, 1), chan_at(3, 1), chan_at(2, 1)
    sent(2)
    gather(3, chan, bot, up, True)
    sent(4)
    gather(5, chan, top, down, True)
    arrived(2, c_down, top)
    gather(6, c_down, top, up)
    arrived(4, c_up, bot)
    gather(7, c_up, bot, down)
    sent(0)
    gather(1, chan, bot, across, True)

    loads["w"].wait()
    loads["tok"].wait()

    def w_of(c):
        return w[pl.ds(pl.multiple_of(c * width, width), width), :]

    acc[...] = mm(tok[chan], w_of(chan))
    arrived(3, c_down, bot)
    acc[...] += mm(tok[c_down], w_of(c_down))
    arrived(5, c_up, top)
    acc[...] += mm(tok[c_up], w_of(c_up))
    arrived(0, o_me, top)
    gather(8, o_me, top, up)
    gather(11, o_me, top, down)

    loads["gk"].wait()
    loads["bias"].wait()
    loads["idft"].wait()
    arrived(8, o_down, top)
    gather(12, o_down, top, up)
    arrived(1, o_me, bot)
    gather(10, o_me, bot, down)
    gather(9, o_me, bot, up)

    col0 = pl.multiple_of((me % n_cg) * lanes, lanes)
    rho = jnp.exp(dec[:, pl.ds(col0, lanes)] * (-block / length))
    landed(0)

    def back(i, r):
        b = groups - 1 - i
        src[1, b] = r.astype(BF)
        return rho * (r + dst[0, b].astype(F32))

    lax.fori_loop(0, groups, back, jnp.zeros((16, lanes), F32), unroll=8)
    spread(1)

    arrived(10, o_up, bot)
    gather(13, o_up, bot, down)

    landed(1)
    unstage(1)
    pspec[pl.ds(0, n_even), :] = (wts[...] * (carry[...] + 0.5 * gspec[pl.ds(0, n_even), :])).astype(BF)
    gc, gsn = gspec[pl.ds(n_even, half), :], gspec[pl.ds(n_even + half, half), :]
    pspec[pl.ds(n_even, half), :] = (inv * (kern_c * gc + kern[...] * gsn)).astype(BF)
    pspec[pl.ds(n_even + half, half), :] = (inv * (kern_c * gsn - kern[...] * gc)).astype(BF)
    gin[...] = grow[...] * mm(idft[...], pspec[...]) + bias[...] * gs[...]
    gval[...] = (gk[...].astype(F32) * gin[...]).astype(BF)

    rs = []

    def reduce_send(i, s, d, target):
        cp = pltpu.make_async_remote_copy(
            src_ref=s, dst_ref=d, send_sem=rs_send.at[i], recv_sem=rs_recv.at[i], device_id=target, device_id_type=MESH,
        )
        cp.start()
        rs.append(cp)

    def reduce_wait(i, r):
        pltpu.make_async_copy(r, r, rs_recv.at[i]).wait()

    def term(p, dy):
        terms[4 * p + dy] = lax.dot_general(gval[...], w_of(chan_at(dy, 1 - p)), NT, preferred_element_type=F32)

    def far_terms(p):
        term(p, 2)
        send_a[p, 0] = terms[4 * p + 2, top].astype(BF)
        send_a[p, 1] = terms[4 * p + 2, bot].astype(BF)
        reduce_send(6 * p, send_a.at[p, 0], got_a.at[p, 0], up)
        reduce_send(6 * p + 1, send_a.at[p, 1], got_a.at[p, 1], down)

    def near_terms(p):
        term(p, 1)
        send_p[p, 0] = terms[4 * p + 1, bot].astype(BF)
        reduce_send(6 * p + 2, send_p.at[p, 0], got_b.at[p, 0, bot], up)
        term(p, 3)
        send_p[p, 1] = terms[4 * p + 3, top].astype(BF)
        reduce_send(6 * p + 3, send_p.at[p, 1], got_b.at[p, 1, top], down)
        term(p, 0)

    def near_sums(p):
        reduce_wait(6 * p, got_a.at[p, 0])
        send_s[p, 0] = (terms[4 * p + 1, top] + got_a[p, 0].astype(F32)).astype(BF)
        reduce_send(6 * p + 4, send_s.at[p, 0], got_b.at[p, 0, top], up)
        reduce_wait(6 * p + 1, got_a.at[p, 1])
        send_s[p, 1] = (terms[4 * p + 3, bot] + got_a[p, 1].astype(F32)).astype(BF)
        reduce_send(6 * p + 5, send_s.at[p, 1], got_b.at[p, 1, bot], down)

    def own_sum(p):
        reduce_wait(6 * p + 2, got_b.at[p, 0, bot])
        reduce_wait(6 * p + 3, got_b.at[p, 1, top])
        reduce_wait(6 * p + 4, got_b.at[p, 0, top])
        reduce_wait(6 * p + 5, got_b.at[p, 1, bot])
        return terms[4 * p] + got_b[p, 0].astype(F32) + got_b[p, 1].astype(F32)

    arrived(6, c_far, top)
    arrived(7, c_far, bot)
    acc[...] += mm(tok[c_far], w_of(c_far))
    acc[...] += mm(tok[o_me], w_of(o_me))
    arrived(9, o_down, bot)
    acc[...] += mm(tok[o_down], w_of(o_down))
    arrived(11, o_up, top)
    acc[...] += mm(tok[o_up], w_of(o_up))
    arrived(12, o_far, top)
    arrived(13, o_far, bot)
    val[...] = (acc[...] + mm(tok[o_far], w_of(o_far))).astype(BF)
    xin[...] = gk[...].astype(F32) * val[...].astype(F32)
    xspec[...] = mm(dft[...], (xin[...] * grow[...]).astype(BF))
    stage(2, xspec)
    spread(2)

    far_terms(0)
    near_terms(0)

    xc, xs = xspec[pl.ds(n_even, half), :], xspec[pl.ds(n_even + half, half), :]
    gc, gsn = gspec[pl.ds(n_even, half), :], gspec[pl.ds(n_even + half, half), :]
    loads["crosst"].wait()
    part = inv * (
        jnp.sum(gc * xc + gsn * xs, axis=0, keepdims=True)
        + jnp.dot(crosst[...], gsn * xc - gc * xs, precision=EXACT, preferred_element_type=F32)
    )
    part_b = jnp.broadcast_to(jnp.sum(xin[...] * gs[...], axis=0, keepdims=True), (8, width))
    for rg in range(n_rg):
        both = jnp.concatenate([part[8 * rg : 8 * rg + 8], part_b]).astype(BF)
        for cg in range(n_cg):
            src[3, rg * n_cg + cg] = both[:, lanes * cg : lanes * cg + lanes]
    spread(3)
    near_sums(0)
    far_terms(1)

    landed(2)

    def fore(b, state):
        z, g_sum = state
        x_b, g_b = dst[2, b].astype(F32), dst[0, b].astype(F32)
        src[4, b] = z.astype(BF)
        prod = g_b * (z + 0.5 * x_b)
        return rho * (z + x_b), g_sum + prod[0:8] + prod[8:16]

    zero = jnp.zeros((16, lanes), F32)
    _, g_sum = lax.fori_loop(0, groups, fore, (zero, jnp.zeros((8, lanes), F32)), unroll=8)
    spread(4)

    landed(3)
    p_sum = jnp.sum(dst[3].astype(F32), axis=0)
    src[5, 0] = jnp.concatenate([(g_sum + p_sum[0:8]) * scale, p_sum[8:16]]).astype(BF)
    dst[5, place(me)] = src[5, 0]
    for i in range(1, side):
        hop(0, src.at[5, 0], dst.at[5, place(me)], z_peer(i))

    send_z[...] = own_sum(0).astype(BF)
    reduce_send(12, send_z, got_z, across)
    near_terms(1)
    near_sums(1)

    hop_wait(0, side - 1)
    mine = pl.ds(dp * seq_size + at_x * side, side)
    for i in range(1, side):
        hop(1, dst.at[5, mine], dst.at[5, mine], x_peer(i))

    landed(4)
    unstage(4)
    pspec[pl.ds(0, n_even), :] = (wts[...] * (carry[...] + 0.5 * xspec[pl.ds(0, n_even), :])).astype(BF)
    pspec[pl.ds(n_even, half), :] = (inv * (kern_c * xc - kern[...] * xs)).astype(BF)
    pspec[pl.ds(n_even + half, half), :] = (inv * (kern_c * xs + kern[...] * xc)).astype(BF)
    state = fade[...] * mm(idft[...], pspec[...]) + bias[...] * xin[...]
    mixed_o[...] = (gq[...].astype(F32) * state).astype(BF)
    gqry_o[...] = (cot[...].astype(F32) * state).astype(BF)
    gkey_o[...] = (val[...].astype(F32) * gin[...]).astype(BF)

    acc[...] = own_sum(1)

    hop_wait(1, side * (side - 1))
    half_of = pl.ds(dp * seq_size, seq_size)
    hop(2, dst.at[5, half_of], dst.at[5, half_of], core_peer)
    hop_wait(2, seq_size)
    for rg in range(n_rg):
        for cg in range(n_cg):
            d = dst[5, place(rg * n_cg + cg)].astype(F32)
            gf_o[pl.ds(8 * rg, 8), pl.ds(lanes * cg, lanes)] = d[0:8]
            if rg == 0:
                gb_o[:, pl.ds(lanes * cg, lanes)] = d[8:9]
    reduce_wait(12, got_z)
    gtok_o[...] = (acc[...] + got_z[...].astype(F32)).astype(BF)

    for trip in range(5):
        left(trip)
    hop_left(0, side - 1)
    hop_left(1, side * (side - 1))
    hop_left(2, seq_size)
    for cp in ag.values():
        cp.wait_send()
    for cp in rs:
        cp.wait_send()


def write_out(*refs):
    copies = [pltpu.make_async_copy(refs[i], refs[6 + i], refs[12].at[i]) for i in range(6)]
    for cp in copies:
        cp.start()
    for cp in copies:
        cp.wait()


def body(tokens, w_value, gate_k, gate_q, filter_weight, decay, skip_bias, cotangent):
    _, block, width = tokens.shape
    seq_size = lax.axis_size("seq")
    groups = seq_size * lax.axis_size("dp")
    chans = lax.axis_size("chan")
    order = filter_weight.shape[0]
    length = block * groups
    half = block // 2
    n_even = 2 * order
    n_spec = n_even + block
    lanes = width * (n_even // 16) // groups
    dft, cross = tables(block, order)
    hbm = pl.BlockSpec(memory_space=pltpu.HBM)
    vmem = pl.BlockSpec(memory_space=pltpu.VMEM)
    wide = (block, width)
    outs = pl.pallas_call(
        functools.partial(kernel, seq_size, length),
        out_shape=[jax.ShapeDtypeStruct(wide, BF)] * 4
        + [jax.ShapeDtypeStruct((order, width), F32), jax.ShapeDtypeStruct((1, width), F32)],
        in_specs=[hbm] * 12,
        out_specs=[vmem] * 6,
        scratch_shapes=[
            pltpu.VMEM((chans, block, width), BF),
            pltpu.VMEM(w_value.shape, BF),
            pltpu.VMEM(wide, BF),
            pltpu.VMEM(wide, BF),
            pltpu.VMEM((order, width), F32),
            pltpu.VMEM(wide, BF),
            pltpu.VMEM((n_spec, block), BF),
            pltpu.VMEM((block, n_spec), BF),
            pltpu.VMEM((half, order), F32),
            pltpu.VMEM((order, half), F32),
            pltpu.VMEM((1, width), F32),
            pltpu.VMEM((1, width), F32),
            pltpu.VMEM(wide, F32),
            pltpu.VMEM(wide, F32),
            pltpu.VMEM(wide, F32),
            pltpu.VMEM(wide, F32),
            pltpu.VMEM(wide, F32),
            pltpu.VMEM(wide, BF),
            pltpu.VMEM(wide, BF),
            pltpu.VMEM(wide, F32),
            pltpu.VMEM((n_spec, width), F32),
            pltpu.VMEM((n_spec, width), F32),
            pltpu.VMEM((n_spec, width), BF),
            pltpu.VMEM((half, width), F32),
            pltpu.VMEM((n_even, width), F32),
            pltpu.VMEM((n_even, width), F32),
            pltpu.VMEM((6, groups, 16, lanes), BF),
            pltpu.VMEM((6, groups, 16, lanes), BF),
            pltpu.VMEM((8, block, width), F32),
            pltpu.VMEM((2, 2, block // 2, width), BF),
            pltpu.VMEM((2, 2, block // 2, width), BF),
            pltpu.VMEM((2, 2, block // 2, width), BF),
            pltpu.VMEM(wide, BF),
            pltpu.VMEM((2, 2, block // 2, width), BF),
            pltpu.VMEM((2, 2, block, width), BF),
            pltpu.VMEM(wide, BF),
            pltpu.SemaphoreType.DMA((12,)),
            pltpu.SemaphoreType.DMA((14,)),
            pltpu.SemaphoreType.DMA((14,)),
            pltpu.SemaphoreType.DMA((13,)),
            pltpu.SemaphoreType.DMA((13,)),
            pltpu.SemaphoreType.DMA((6,)),
            pltpu.SemaphoreType.DMA((6,)),
            pltpu.SemaphoreType.DMA((6,)),
            pltpu.SemaphoreType.DMA((6,)),
        ],
        compiler_params=pltpu.CompilerParams(
            collective_id=0, has_side_effects=True, vmem_limit_bytes=60 * 2**20
        ),
        name="hyena",
    )(
        tokens[0], w_value, gate_k[0], gate_q[0], filter_weight, cotangent[0],
        jnp.asarray(dft, BF), jnp.asarray(dft.T, BF), jnp.asarray(cross), jnp.asarray(cross.T),
        decay[None], skip_bias[None],
    )
    mixed, gtok, gkey, gqry, gfil, gbias = pl.pallas_call(
        write_out,
        out_shape=[jax.ShapeDtypeStruct(o.shape, o.dtype) for o in outs],
        in_specs=[vmem] * 6,
        out_specs=[hbm] * 6,
        scratch_shapes=[pltpu.SemaphoreType.DMA((6,))],
        compiler_params=pltpu.CompilerParams(vmem_limit_bytes=60 * 2**20),
        name="write_out",
    )(*outs)
    return mixed[None], gtok[None], gkey[None], gqry[None], gfil, gbias[0]


def solution(mesh):
    rows = P(None, ("dp", "seq"), "chan")
    cols = P(None, "chan")
    return jax.shard_map(
        body,
        mesh=mesh,
        in_specs=(rows, cols, rows, rows, cols, P("chan"), P("chan"), rows),
        out_specs=(rows, rows, rows, rows, cols, P("chan")),
        check_vma=False,
    )
```

```python
import functools
import math

import jax
import jax.numpy as jnp
import numpy as np
from jax import lax
from jax.experimental import pallas as pl
from jax.experimental.pallas import tpu as pltpu
from jax.sharding import PartitionSpec as P

BF = jnp.bfloat16
F32 = jnp.float32
MESH = pl.DeviceIdType.MESH
EXACT = lax.Precision.HIGHEST
NT = (((1,), (1,)), ((), ()))


def tables(block, order):
    pos = np.arange(block, dtype=np.float64)
    harm = 2.0 * np.pi / block * np.arange(1, order + 1, dtype=np.float64)
    half = np.pi / block * (2.0 * np.arange(block // 2, dtype=np.float64) + 1.0)
    even = harm[:, None] * pos[None, :]
    odd = half[:, None] * pos[None, :]
    pair = np.stack([np.cos(even).reshape(-1, 8, block), np.sin(even).reshape(-1, 8, block)], 1)
    dft = np.concatenate([pair.reshape(2 * order, block), np.cos(odd), np.sin(odd)])
    cross = np.sin(odd) @ np.cos(even).T
    return dft.astype(np.float32), cross.astype(np.float32)


def mm(a, b):
    return jnp.dot(a, b, preferred_element_type=F32)


def kernel(
    seq_size, length,
    tok_h, w_h, gk_h, gq_h, fw_h, cot_h, dft_h, idft_h, cross_h, crosst_h, dec_h, bias_h,
    mixed_o, gtok_o, gkey_o, gqry_o, gf_o, gb_o,
    tok, w, gk, gq, fw, cot, dft, idft, cross, crosst, dec, bias,
    fade, grow, gs, gin, xin, val, gval, acc, gspec, xspec, pspec, kern, wts, carry,
    src, dst, terms, send_a, send_p, send_s, send_z, got_a, got_b, got_z,
    load_sem, ag_send, ag_recv, rs_send, rs_recv, st_send, st_recv, hop_send, hop_recv,
):
    block, width = gk.shape
    rows = block // 2
    order = fw.shape[0]
    groups = 2 * seq_size
    n_even = 2 * order
    half = block // 2
    lanes = src.shape[3]
    n_rg = n_even // 16
    n_cg = width // lanes
    scale = 1.0 / math.sqrt(order * length)
    inv = 1.0 / block

    dp, seq, chan = lax.axis_index("dp"), lax.axis_index("seq"), lax.axis_index("chan")
    me = dp * seq_size + seq
    y, zh = chan // 2, chan % 2

    def chan_at(dy, other):
        return ((y + dy) % 4) * 2 + (zh + other) % 2

    def at_chan(c):
        return (dp, seq, c)

    up, down, across = at_chan(chan_at(1, 0)), at_chan(chan_at(3, 0)), at_chan(chan_at(0, 1))

    def peer(i):
        b = (me + i) % groups
        return b, (b // seq_size, b % seq_size, chan)

    barrier = pltpu.get_barrier_semaphore()
    for target in (up, down, across):
        pl.semaphore_signal(barrier, inc=1, device_id=target, device_id_type=MESH)

    def greet(i, carry_):
        pl.semaphore_signal(barrier, inc=1, device_id=peer(i)[1], device_id_type=MESH)
        return carry_

    lax.fori_loop(1, groups, greet, 0)
    loads = {}
    order_of = [
        ("gq", gq_h, gq), ("cot", cot_h, cot), ("dec", dec_h, dec), ("dft", dft_h, dft), ("fw", fw_h, fw), ("cross", cross_h, cross),
        ("gk", gk_h, gk), ("idft", idft_h, idft), ("crosst", crosst_h, crosst), ("w", w_h, w),
        ("tok", tok_h, tok.at[chan]), ("bias", bias_h, bias),
    ]
    for i, (name, a, b) in enumerate(order_of):
        loads[name] = pltpu.make_async_copy(a, b, load_sem.at[i])
        loads[name].start()
    def stage(trip, ref):
        for rg in range(n_rg):
            for cg in range(n_cg):
                src[trip, rg * n_cg + cg] = ref[pl.ds(16 * rg, 16), pl.ds(lanes * cg, lanes)].astype(BF)

    pl.semaphore_wait(barrier, groups + 2)

    top, bot = pl.ds(0, rows), pl.ds(rows, rows)

    ag = {}

    def gather(i, slot, part, target, first=False):
        s = tok_h.at[part] if first else tok.at[slot, part]
        cp = pltpu.make_async_remote_copy(
            src_ref=s, dst_ref=tok.at[slot, part], send_sem=ag_send.at[i], recv_sem=ag_recv.at[i],
            device_id=target, device_id_type=MESH,
        )
        cp.start()
        ag[i] = cp

    def arrived(i, slot, part):
        r = tok.at[slot, part]
        pltpu.make_async_copy(r, r, ag_recv.at[i]).wait()

    def sent(i):
        ag.pop(i).wait_send()

    gather(0, chan, top, across, True)
    gather(2, chan, top, up, True)
    gather(4, chan, bot, down, True)

    def spread(trip):
        def one(i, carry_):
            b, target = peer(i)
            s = src.at[trip, b]
            pltpu.make_async_remote_copy(
                src_ref=s, dst_ref=dst.at[trip, me], send_sem=st_send.at[trip], recv_sem=st_recv.at[trip],
                device_id=target, device_id_type=MESH,
            ).start()
            return carry_

        lax.fori_loop(1, groups, one, 0, unroll=True)
        dst[trip, me] = src[trip, me]

    side = 4
    at_x, at_z = seq % side, seq // side

    def place(b):
        return (b // seq_size) * seq_size + (b % side) * side + (b % seq_size) // side

    def hop(step, s, d, target):
        pltpu.make_async_remote_copy(
            src_ref=s, dst_ref=d, send_sem=hop_send.at[step], recv_sem=hop_recv.at[step],
            device_id=target, device_id_type=MESH,
        ).start()

    def hop_wait(step, n):
        r = dst.at[5, pl.ds(0, n)]
        pltpu.make_async_copy(r, r, hop_recv.at[step]).wait()

    def hop_left(step, n):
        r = dst.at[5, pl.ds(0, n)]
        pltpu.make_async_copy(r, r, hop_send.at[step]).wait()

    def z_peer(i):
        return (dp, ((at_z + i) % side) * side + at_x, chan)

    def x_peer(i):
        return (dp, at_z * side + (at_x + i) % side, chan)

    core_peer = (1 - dp, seq, chan)

    def landed(trip):
        r = dst.at[trip, pl.ds(0, groups - 1)]
        pltpu.make_async_copy(r, r, st_recv.at[trip]).wait()

    def left(trip):
        r = src.at[trip, pl.ds(0, groups - 1)]
        pltpu.make_async_copy(r, r, st_send.at[trip]).wait()

    def unstage(trip):
        for rg in range(n_rg):
            for cg in range(n_cg):
                carry[pl.ds(16 * rg, 16), pl.ds(lanes * cg, lanes)] = dst[trip, rg * n_cg + cg].astype(F32)

    loads["gq"].wait()
    loads["cot"].wait()
    loads["dec"].wait()
    pos = lax.broadcasted_iota(jnp.int32, (block, width), 0).astype(F32) * (1.0 / length)
    rate = pos * dec[...]
    fade[...] = jnp.exp(-rate)
    grow[...] = jnp.exp(rate)
    gs[...] = gq[...].astype(F32) * cot[...].astype(F32)
    loads["dft"].wait()
    gspec[...] = mm(dft[...], (gs[...] * fade[...]).astype(BF))
    stage(0, gspec)
    spread(0)
    loads["fw"].wait()
    loads["cross"].wait()
    scaled = fw[...] * scale
    for rg in range(n_rg):
        eight = scaled[8 * rg : 8 * rg + 8]
        wts[pl.ds(16 * rg, 8), :] = eight
        wts[pl.ds(16 * rg + 8, 8), :] = eight
    kern[...] = jnp.dot(cross[...], scaled, precision=EXACT, preferred_element_type=F32)
    kern_c = jnp.sum(scaled, axis=0, keepdims=True)


    c_up, c_down, c_far = chan_at(1, 0), chan_at(3, 0), chan_at(2, 0)
    o_me, o_up, o_down, o_far = chan_at(0, 1), chan_at(1, 1), chan_at(3, 1), chan_at(2, 1)
    sent(2)
    gather(3, chan, bot, up, True)
    sent(4)
    gather(5, chan, top, down, True)
    arrived(2, c_down, top)
    gather(6, c_down, top, up)
    arrived(4, c_up, bot)
    gather(7, c_up, bot, down)
    sent(0)
    gather(1, chan, bot, across, True)

    loads["w"].wait()
    loads["tok"].wait()

    def w_of(c):
        return w[pl.ds(pl.multiple_of(c * width, width), width), :]

    acc[...] = mm(tok[chan], w_of(chan))
    arrived(3, c_down, bot)
    acc[...] += mm(tok[c_down], w_of(c_down))
    arrived(5, c_up, top)
    acc[...] += mm(tok[c_up], w_of(c_up))
    arrived(0, o_me, top)
    gather(8, o_me, top, up)
    gather(11, o_me, top, down)

    loads["gk"].wait()
    loads["bias"].wait()
    loads["idft"].wait()
    arrived(8, o_down, top)
    gather(12, o_down, top, up)
    arrived(1, o_me, bot)
    gather(10, o_me, bot, down)
    gather(9, o_me, bot, up)

    col0 = pl.multiple_of((me % n_cg) * lanes, lanes)
    rho = jnp.exp(dec[:, pl.ds(col0, lanes)] * (-block / length))
    landed(0)

    def back(i, r):
        b = groups - 1 - i
        src[1, b] = r.astype(BF)
        return rho * (r + dst[0, b].astype(F32))

    lax.fori_loop(0, groups, back, jnp.zeros((16, lanes), F32), unroll=8)
    spread(1)

    arrived(10, o_up, bot)
    gather(13, o_up, bot, down)

    landed(1)
    unstage(1)
    pspec[pl.ds(0, n_even), :] = (wts[...] * (carry[...] + 0.5 * gspec[pl.ds(0, n_even), :])).astype(BF)
    gc, gsn = gspec[pl.ds(n_even, half), :], gspec[pl.ds(n_even + half, half), :]
    pspec[pl.ds(n_even, half), :] = (inv * (kern_c * gc + kern[...] * gsn)).astype(BF)
    pspec[pl.ds(n_even + half, half), :] = (inv * (kern_c * gsn - kern[...] * gc)).astype(BF)
    gin[...] = grow[...] * mm(idft[...], pspec[...]) + bias[...] * gs[...]
    gval[...] = (gk[...].astype(F32) * gin[...]).astype(BF)

    rs = []

    def reduce_send(i, s, d, target):
        cp = pltpu.make_async_remote_copy(
            src_ref=s, dst_ref=d, send_sem=rs_send.at[i], recv_sem=rs_recv.at[i], device_id=target, device_id_type=MESH,
        )
        cp.start()
        rs.append(cp)

    def reduce_wait(i, r):
        pltpu.make_async_copy(r, r, rs_recv.at[i]).wait()

    def term(p, dy):
        terms[4 * p + dy] = lax.dot_general(gval[...], w_of(chan_at(dy, 1 - p)), NT, preferred_element_type=F32)

    def far_terms(p):
        term(p, 2)
        send_a[p, 0] = terms[4 * p + 2, top].astype(BF)
        send_a[p, 1] = terms[4 * p + 2, bot].astype(BF)
        reduce_send(6 * p, send_a.at[p, 0], got_a.at[p, 0], up)
        reduce_send(6 * p + 1, send_a.at[p, 1], got_a.at[p, 1], down)

    def near_terms(p):
        term(p, 1)
        send_p[p, 0] = terms[4 * p + 1, bot].astype(BF)
        reduce_send(6 * p + 2, send_p.at[p, 0], got_b.at[p, 0, bot], up)
        term(p, 3)
        send_p[p, 1] = terms[4 * p + 3, top].astype(BF)
        reduce_send(6 * p + 3, send_p.at[p, 1], got_b.at[p, 1, top], down)
        term(p, 0)

    def near_sums(p):
        reduce_wait(6 * p, got_a.at[p, 0])
        send_s[p, 0] = (terms[4 * p + 1, top] + got_a[p, 0].astype(F32)).astype(BF)
        reduce_send(6 * p + 4, send_s.at[p, 0], got_b.at[p, 0, top], up)
        reduce_wait(6 * p + 1, got_a.at[p, 1])
        send_s[p, 1] = (terms[4 * p + 3, bot] + got_a[p, 1].astype(F32)).astype(BF)
        reduce_send(6 * p + 5, send_s.at[p, 1], got_b.at[p, 1, bot], down)

    def own_sum(p):
        reduce_wait(6 * p + 2, got_b.at[p, 0, bot])
        reduce_wait(6 * p + 3, got_b.at[p, 1, top])
        reduce_wait(6 * p + 4, got_b.at[p, 0, top])
        reduce_wait(6 * p + 5, got_b.at[p, 1, bot])
        return terms[4 * p] + got_b[p, 0].astype(F32) + got_b[p, 1].astype(F32)

    arrived(6, c_far, top)
    arrived(7, c_far, bot)
    acc[...] += mm(tok[c_far], w_of(c_far))
    acc[...] += mm(tok[o_me], w_of(o_me))
    arrived(9, o_down, bot)
    acc[...] += mm(tok[o_down], w_of(o_down))
    arrived(11, o_up, top)
    acc[...] += mm(tok[o_up], w_of(o_up))
    arrived(12, o_far, top)
    arrived(13, o_far, bot)
    val[...] = (acc[...] + mm(tok[o_far], w_of(o_far))).astype(BF)
    xin[...] = gk[...].astype(F32) * val[...].astype(F32)
    xspec[...] = mm(dft[...], (xin[...] * grow[...]).astype(BF))
    stage(2, xspec)
    spread(2)

    far_terms(0)
    near_terms(0)

    xc, xs = xspec[pl.ds(n_even, half), :], xspec[pl.ds(n_even + half, half), :]
    gc, gsn = gspec[pl.ds(n_even, half), :], gspec[pl.ds(n_even + half, half), :]
    loads["crosst"].wait()
    part = inv * (
        jnp.sum(gc * xc + gsn * xs, axis=0, keepdims=True)
        + jnp.dot(crosst[...], gsn * xc - gc * xs, precision=EXACT, preferred_element_type=F32)
    )
    part_b = jnp.broadcast_to(jnp.sum(xin[...] * gs[...], axis=0, keepdims=True), (8, width))
    for rg in range(n_rg):
        both = jnp.concatenate([part[8 * rg : 8 * rg + 8], part_b]).astype(BF)
        for cg in range(n_cg):
            src[3, rg * n_cg + cg] = both[:, lanes * cg : lanes * cg + lanes]
    spread(3)
    near_sums(0)
    far_terms(1)

    landed(2)

    def fore(b, state):
        z, g_sum = state
        x_b, g_b = dst[2, b].astype(F32), dst[0, b].astype(F32)
        src[4, b] = z.astype(BF)
        prod = g_b * (z + 0.5 * x_b)
        return rho * (z + x_b), g_sum + prod[0:8] + prod[8:16]

    zero = jnp.zeros((16, lanes), F32)
    _, g_sum = lax.fori_loop(0, groups, fore, (zero, jnp.zeros((8, lanes), F32)), unroll=8)
    spread(4)

    landed(3)
    p_sum = jnp.sum(dst[3].astype(F32), axis=0)
    src[5, 0] = jnp.concatenate([(g_sum + p_sum[0:8]) * scale, p_sum[8:16]]).astype(BF)
    dst[5, place(me)] = src[5, 0]
    for i in range(1, side):
        hop(0, src.at[5, 0], dst.at[5, place(me)], z_peer(i))

    send_z[...] = own_sum(0).astype(BF)
    reduce_send(12, send_z.at[top], got_z.at[top], across)
    reduce_send(13, send_z.at[bot], got_z.at[bot], across)
    near_terms(1)
    near_sums(1)

    hop_wait(0, side - 1)
    mine = pl.ds(dp * seq_size + at_x * side, side)
    for i in range(1, side):
        hop(1, dst.at[5, mine], dst.at[5, mine], x_peer(i))

    landed(4)
    unstage(4)
    pspec[pl.ds(0, n_even), :] = (wts[...] * (carry[...] + 0.5 * xspec[pl.ds(0, n_even), :])).astype(BF)
    pspec[pl.ds(n_even, half), :] = (inv * (kern_c * xc - kern[...] * xs)).astype(BF)
    pspec[pl.ds(n_even + half, half), :] = (inv * (kern_c * xs + kern[...] * xc)).astype(BF)
    state = fade[...] * mm(idft[...], pspec[...]) + bias[...] * xin[...]
    mixed_o[...] = (gq[...].astype(F32) * state).astype(BF)
    gqry_o[...] = (cot[...].astype(F32) * state).astype(BF)
    gkey_o[...] = (val[...].astype(F32) * gin[...]).astype(BF)

    acc[...] = own_sum(1)

    hop_wait(1, side * (side - 1))
    half_of = pl.ds(dp * seq_size, seq_size)
    hop(2, dst.at[5, half_of], dst.at[5, half_of], core_peer)
    hop_wait(2, seq_size)
    for rg in range(n_rg):
        for cg in range(n_cg):
            d = dst[5, place(rg * n_cg + cg)].astype(F32)
            gf_o[pl.ds(8 * rg, 8), pl.ds(lanes * cg, lanes)] = d[0:8]
            if rg == 0:
                gb_o[:, pl.ds(lanes * cg, lanes)] = d[8:9]
    for i, part in ((12, top), (13, bot)):
        reduce_wait(i, got_z.at[part])
        gtok_o[part, :] = (acc[part, :] + got_z[part, :].astype(F32)).astype(BF)

    for trip in range(5):
        left(trip)
    hop_left(0, side - 1)
    hop_left(1, side * (side - 1))
    hop_left(2, seq_size)
    for cp in ag.values():
        cp.wait_send()
    for cp in rs:
        cp.wait_send()


def write_out(*refs):
    copies = [pltpu.make_async_copy(refs[i], refs[6 + i], refs[12].at[i]) for i in range(6)]
    for cp in copies:
        cp.start()
    for cp in copies:
        cp.wait()


def body(tokens, w_value, gate_k, gate_q, filter_weight, decay, skip_bias, cotangent):
    _, block, width = tokens.shape
    seq_size = lax.axis_size("seq")
    groups = seq_size * lax.axis_size("dp")
    chans = lax.axis_size("chan")
    order = filter_weight.shape[0]
    length = block * groups
    half = block // 2
    n_even = 2 * order
    n_spec = n_even + block
    lanes = width * (n_even // 16) // groups
    dft, cross = tables(block, order)
    hbm = pl.BlockSpec(memory_space=pltpu.HBM)
    vmem = pl.BlockSpec(memory_space=pltpu.VMEM)
    wide = (block, width)
    outs = pl.pallas_call(
        functools.partial(kernel, seq_size, length),
        out_shape=[jax.ShapeDtypeStruct(wide, BF)] * 4
        + [jax.ShapeDtypeStruct((order, width), F32), jax.ShapeDtypeStruct((1, width), F32)],
        in_specs=[hbm] * 12,
        out_specs=[vmem] * 6,
        scratch_shapes=[
            pltpu.VMEM((chans, block, width), BF),
            pltpu.VMEM(w_value.shape, BF),
            pltpu.VMEM(wide, BF),
            pltpu.VMEM(wide, BF),
            pltpu.VMEM((order, width), F32),
            pltpu.VMEM(wide, BF),
            pltpu.VMEM((n_spec, block), BF),
            pltpu.VMEM((block, n_spec), BF),
            pltpu.VMEM((half, order), F32),
            pltpu.VMEM((order, half), F32),
            pltpu.VMEM((1, width), F32),
            pltpu.VMEM((1, width), F32),
            pltpu.VMEM(wide, F32),
            pltpu.VMEM(wide, F32),
            pltpu.VMEM(wide, F32),
            pltpu.VMEM(wide, F32),
            pltpu.VMEM(wide, F32),
            pltpu.VMEM(wide, BF),
            pltpu.VMEM(wide, BF),
            pltpu.VMEM(wide, F32),
            pltpu.VMEM((n_spec, width), F32),
            pltpu.VMEM((n_spec, width), F32),
            pltpu.VMEM((n_spec, width), BF),
            pltpu.VMEM((half, width), F32),
            pltpu.VMEM((n_even, width), F32),
            pltpu.VMEM((n_even, width), F32),
            pltpu.VMEM((6, groups, 16, lanes), BF),
            pltpu.VMEM((6, groups, 16, lanes), BF),
            pltpu.VMEM((8, block, width), F32),
            pltpu.VMEM((2, 2, block // 2, width), BF),
            pltpu.VMEM((2, 2, block // 2, width), BF),
            pltpu.VMEM((2, 2, block // 2, width), BF),
            pltpu.VMEM(wide, BF),
            pltpu.VMEM((2, 2, block // 2, width), BF),
            pltpu.VMEM((2, 2, block, width), BF),
            pltpu.VMEM(wide, BF),
            pltpu.SemaphoreType.DMA((12,)),
            pltpu.SemaphoreType.DMA((14,)),
            pltpu.SemaphoreType.DMA((14,)),
            pltpu.SemaphoreType.DMA((14,)),
            pltpu.SemaphoreType.DMA((14,)),
            pltpu.SemaphoreType.DMA((6,)),
            pltpu.SemaphoreType.DMA((6,)),
            pltpu.SemaphoreType.DMA((6,)),
            pltpu.SemaphoreType.DMA((6,)),
        ],
        compiler_params=pltpu.CompilerParams(
            collective_id=0, has_side_effects=True, vmem_limit_bytes=60 * 2**20
        ),
        name="hyena",
    )(
        tokens[0], w_value, gate_k[0], gate_q[0], filter_weight, cotangent[0],
        jnp.asarray(dft, BF), jnp.asarray(dft.T, BF), jnp.asarray(cross), jnp.asarray(cross.T),
        decay[None], skip_bias[None],
    )
    mixed, gtok, gkey, gqry, gfil, gbias = pl.pallas_call(
        write_out,
        out_shape=[jax.ShapeDtypeStruct(o.shape, o.dtype) for o in outs],
        in_specs=[vmem] * 6,
        out_specs=[hbm] * 6,
        scratch_shapes=[pltpu.SemaphoreType.DMA((6,))],
        compiler_params=pltpu.CompilerParams(vmem_limit_bytes=60 * 2**20),
        name="write_out",
    )(*outs)
    return mixed[None], gtok[None], gkey[None], gqry[None], gfil, gbias[0]


def solution(mesh):
    rows = P(None, ("dp", "seq"), "chan")
    cols = P(None, "chan")
    return jax.shard_map(
        body,
        mesh=mesh,
        in_specs=(rows, cols, rows, rows, cols, P("chan"), P("chan"), rows),
        out_specs=(rows, rows, rows, rows, cols, P("chan")),
        check_vma=False,
    )
```
